128 devices in a mesh: occ: 8 (over z_lo, x), vir: 16 (over z_hi, y, core).
Axes of the slice: x: 4, y: 4, z: 4 (z_hi: 2, z_lo: 2; z = z_hi * 2 + z_lo), core: 2. Of those that a mesh axis runs over, the one named last changes fastest.
Arguments:
- integrals: float32 [2048, 130816], P('occ', 'vir'), may hold values from -0.0234375 to 0.0234375
- amplitudes: float32 [2016, 130816], P('occ', 'vir'), may hold values from -6 to 6
- residual_in: float32 [2016, 2048], P('occ', 'vir'), may hold values from -6 to 6
Outputs:
- residual_out: float32 [2016, 2048], P('occ', 'vir')
The draws below stay inside these ranges and needn't reach their ends.
All inputs are finite; a program needn't handle non-finite values.
Results may differ from the reference program's by a relative error of at most 0.000075.
Values sent between devices are 32-bit elements; how exact they have to be, the bound alone decides.
A program may use at most 128 MiB of HBM per device.

```python
import jax
import jax.numpy as jnp
from jax import lax

AB = 2048
CD = 130816
IJ = 2016


def strengthened(entries, key, source, target, blocks, factor):
    owner, partner = [(jnp.arange(entries.shape[position]) // (entries.shape[position] // blocks)).reshape([-1 if axis == position else 1 for axis in range(entries.ndim)]) for position in (source, target)]
    chosen = jax.random.permutation(key, blocks)[partner]
    strong = (owner == chosen) | (owner == (partner + blocks // 2) % blocks)
    return jnp.where(strong, factor * entries, entries)


def block_scale(key, dims, cuts, least, high):
    loudness = 1.0
    for axis_at, shards_of in cuts:
        steps = jax.random.uniform(jax.random.fold_in(jax.random.fold_in(key, 6), axis_at), (shards_of,), jnp.float32, least / len(cuts), high / len(cuts))
        loudness = loudness * jnp.repeat(jnp.exp(steps), dims[axis_at] // shards_of).reshape((-1,) + (1,) * (len(dims) - 1 - axis_at))
    return loudness


def noise(own_key, shape, scale, reach, shards=(), dtype=jnp.bfloat16):
    factor_of = block_scale(own_key, shape, shards, -0.22, 0.18) if shards else 1.0
    array = jax.random.normal(own_key, shape, jnp.float32) * scale * factor_of
    return jnp.minimum(jnp.maximum(array, -reach), reach).astype(dtype)


def bell_draw_with(rng, shape, scale, limit, pieces, heavy, dtype=jnp.bfloat16):
    result = scale * jax.random.normal(rng, shape, jnp.float32)
    if pieces:
        result = result * block_scale(rng, shape, pieces, -0.22, 0.18)
    return jnp.clip(strengthened(result, jax.random.fold_in(rng, 3), *heavy), -limit, limit).astype(dtype)


def setup_inputs(seed: int = 0) -> dict:
    key_of = jax.random.split(jax.random.key(seed), 4)
    integrals = bell_draw_with(key_of[0], (AB, CD), CD ** -0.5, 0.0234375, ((0, 8), (1, 16)), (1, 0, 16, 2.0), jnp.float32)
    amplitudes = noise(key_of[1], (IJ, CD), 1.0, 6.0, ((0, 8), (1, 16)), jnp.float32)
    residual_in = noise(key_of[2], (IJ, AB), 1.0, 6.0, ((0, 8), (1, 16)), jnp.float32)
    return dict(integrals=integrals, amplitudes=amplitudes, residual_in=residual_in)


def reference(integrals, amplitudes, residual_in):
    ladder = lax.dot_general(amplitudes, integrals, (((1,), (1,)), ((), ())), precision=lax.Precision.HIGHEST, preferred_element_type=jnp.float32)
    return residual_in + ladder
```

```python
import jax
import jax.numpy as jnp
from jax import lax
from jax.experimental import pallas as pl
from jax.experimental.pallas import tpu as pltpu
from jax.sharding import PartitionSpec as P

MESH = pl.DeviceIdType.MESH
F32, BF16 = jnp.float32, jnp.bfloat16
NT = (((1,), (1,)), ((), ()))

ROWS, HALF, QUARTER, LANES = 256, 128, 2048, 128
SLOTS = 8

OFFSET = (0, -1, 1, 2)


def dot(a, b):
    return lax.dot_general(a, b, NT, preferred_element_type=F32)


def kernel(
    amp, amp_cols, amp_rows, itg, itg_cols, residual, out,
    vx, vz, ax, stage, vhi, vlo, ahi, alo, ptile, crecv, yrecv, xrecv, total, zsend, zrecv,
    own_sem, gsend, grecv_v, grecv_a, fsend, frecv, csend, crecv_sem, ysend, yrecv_sem,
    osend, orecv, zsem,
):
    occ, vir = lax.axis_index("occ"), lax.axis_index("vir")
    x, zl = lax.rem(occ, 4), occ // 4
    core, y, zh = lax.rem(vir, 2), lax.rem(vir // 2, 4), vir // 8

    def at(dx=0, dzl=0, dy=0, dzh=0, dc=0):
        return (
            lax.rem(zl + dzl, 2) * 4 + lax.rem(x + dx + 4, 4),
            lax.rem(zh + dzh, 2) * 8 + lax.rem(y + dy + 4, 4) * 2 + lax.rem(core + dc, 2),
        )

    peers = [at(dx=1), at(dx=-1), at(dx=2), at(dzl=1), at(dc=1), at(dy=1), at(dy=-1), at(dy=2), at(dzh=1)]
    barrier = pltpu.get_barrier_semaphore()
    for peer in peers:
        pl.semaphore_signal(barrier, inc=1, device_id=peer, device_id_type=MESH)
    pl.semaphore_wait(barrier, len(peers))

    def remote(src, dst, ssem, rsem, device):
        pltpu.make_async_remote_copy(
            src_ref=src, dst_ref=dst, send_sem=ssem, recv_sem=rsem, device_id=device, device_id_type=MESH
        ).start()

    def wait(ref, sem):
        pltpu.make_async_copy(ref, ref, sem).wait()

    def spread(array, cols, rows, half, quarter, dst, make):
        r0 = half * HALF
        n = HALF if rows is None or half == 0 else HALF - 8

        @pl.when(quarter != 3)
        def _():
            at_col = pl.multiple_of(quarter * QUARTER, LANES)
            make(array.at[pl.ds(r0, n), pl.ds(at_col, QUARTER)], dst.at[pl.ds(0, n)])

        @pl.when(quarter == 3)
        def _():
            main = QUARTER - LANES
            make(array.at[pl.ds(r0, n), pl.ds(3 * QUARTER, main)], dst.at[pl.ds(0, n), pl.ds(0, main)])
            make(cols.at[pl.ds(r0, n)], dst.at[pl.ds(0, n), pl.ds(main, LANES)])

        if n != HALF:
            at_col = pl.multiple_of(quarter * QUARTER, LANES)
            make(rows.at[:, pl.ds(at_col, QUARTER)], dst.at[pl.ds(n, 8)])

    def send(kind, half, dx, s):
        quarter = lax.rem(x + dx + 4, 4)
        device = at(dx=dx)
        if kind == "v":
            ssem, rsem = gsend.at[s, half], grecv_v.at[s, half]
            spread(itg, itg_cols, None, half, quarter, vx.at[s, half], lambda a, b: remote(a, b, ssem, rsem, device))
        else:
            ssem, rsem = gsend.at[s, 2 + half], grecv_a.at[s, half]
            dst = ax.at[s, pl.ds(half * HALF, HALF)]
            spread(amp, amp_cols, amp_rows, half, quarter, dst, lambda a, b: remote(a, b, ssem, rsem, device))

    def send_near(kind, half):
        send(kind, half, 1, 0)
        send(kind, half, -1, 1)

    def send_far(kind, half):
        send(kind, half, 2, 2)

    def forward(s, half):
        remote(vx.at[s, half], vz.at[s + 1, half], fsend.at[s + 1, half], frecv.at[s + 1, half], at(dzl=1))

    def split(src, hi, lo):
        def step(c, _):
            rows = pl.ds(pl.multiple_of(c * 32, 32), 32)
            value = src[rows]
            high = value.astype(BF16)
            hi[rows] = high
            lo[rows] = (value - high.astype(F32)).astype(BF16)
            return 0

        lax.fori_loop(0, HALF // 32, step, 0)

    def split_v(src, j, half):
        rows = pl.ds(half * HALF, HALF)
        split(src, vhi.at[j, rows], vlo.at[j, rows])

    def split_a(src, i, half):
        rows = pl.ds(half * HALF, HALF)
        split(src, ahi.at[i, rows], alo.at[i, rows])

    def take_v(s, half):
        wait(vx.at[s, half], grecv_v.at[s, half])
        forward(s, half)

    def take_z(s, half):
        wait(vz.at[s, half], frecv.at[s, half])
        split_v(vz.at[s, half], 4 + s, half)

    def take_a(s, half):
        rows = pl.ds(half * HALF, HALF)
        wait(ax.at[s, rows], grecv_a.at[s, half])
        split_a(ax.at[s, rows], s + 1, half)

    def rows_of(half):
        return pl.ds(0, ROWS) if half is None else pl.ds(half * HALF, HALF)

    def sem_row(i, half):
        return i if half is None else 3 + half

    def produce(i, j, half, slot, free):
        rows = rows_of(half)
        n = ROWS if half is None else HALF
        if not free:
            wait(ptile.at[slot, 0, pl.ds(0, n)], csend.at[slot])
        high, low = ahi[i, rows], alo[i, rows]
        both = jnp.concatenate([high, low], axis=0)
        one = dot(both, vhi[j])
        if half is None:
            value = one[:n] + one[n:] + dot(high, vlo[j])
        else:
            two = dot(both, vlo[j])
            value = one[:n] + one[n:] + two[:n] + two[n:]
        ptile[slot, 0, pl.ds(0, n)] = value[:, :LANES]
        ptile[slot, 1, pl.ds(0, n)] = value[:, LANES:]
        remote(
            ptile.at[slot, 1 - core, pl.ds(0, n)], crecv.at[j, i, rows],
            csend.at[slot], crecv_sem.at[j, sem_row(i, half)], at(dc=1),
        )

    def finish(i, j, half, slot):
        rows = rows_of(half)
        n = ROWS if half is None else HALF
        wait(crecv.at[j, i, rows], crecv_sem.at[j, sem_row(i, half)])
        crecv[j, i, rows] += ptile[slot, core, pl.ds(0, n)]
        d, zj = lax.rem(j, 4), j // 4
        shift = jnp.where(d == 0, 4, jnp.where(d == 1, 3, jnp.where(d == 2, 5, 6)))
        target = lax.rem(x + shift, 4)
        distance = lax.rem(y - target + 4, 4)

        @pl.when(distance != 0)
        def _():
            remote(
                crecv.at[j, i, rows], yrecv.at[distance - 1, zj, i, rows],
                ysend, yrecv_sem.at[distance - 1, zj, sem_row(i, half)],
                (occ, zh * 8 + target * 2 + core),
            )

    def tiles(count, n, index, half=None, free=False):
        def step(k, _):
            @pl.when(k < n)
            def _():
                i, j = index(k)
                produce(i, j, half, lax.rem(count + k, SLOTS), free)

            @pl.when(k > 0)
            def _():
                i, j = index(k - 1)
                finish(i, j, half, lax.rem(count + k - 1, SLOTS))

            return 0

        lax.fori_loop(0, n + 1, step, 0)

    def settle(n):
        for slot in range(SLOTS):
            wait(ptile.at[slot, 0, pl.ds(0, n)], csend.at[slot])

    send_near("v", 0)
    send_near("v", 1)
    for half in range(2):
        spread(
            itg, itg_cols, None, half, x, vz.at[0, half],
            lambda a, b, half=half: remote(a, b, fsend.at[0, half], frecv.at[0, half], at(dzl=1)),
        )
    for half in range(2):
        spread(itg, itg_cols, None, half, x, stage.at[half], lambda a, b, half=half: pltpu.make_async_copy(a, b, own_sem.at[half]).start())
    for half in range(2):
        wait(stage.at[half], own_sem.at[half])
        split_v(stage.at[half], 0, half)
        spread(amp, amp_cols, amp_rows, half, x, stage.at[half], lambda a, b, half=half: pltpu.make_async_copy(a, b, own_sem.at[half]).start())
    for half in range(2):
        wait(stage.at[half], own_sem.at[half])
        split_a(stage.at[half], 0, half)

    take_v(0, 0)
    take_v(1, 0)
    send_near("a", 0)
    split_v(vx.at[0, 0], 1, 0)
    split_v(vx.at[1, 0], 2, 0)
    take_z(0, 0)

    take_v(0, 1)
    take_v(1, 1)
    send_near("a", 1)
    split_v(vx.at[0, 1], 1, 1)
    split_v(vx.at[1, 1], 2, 1)
    take_z(0, 1)
    tiles(0, 4, lambda k: (0, k + k // 3), free=True)

    take_a(0, 0)
    take_a(1, 0)
    send_far("v", 0)
    take_z(1, 0)

    take_a(0, 1)
    take_a(1, 1)
    send_far("v", 1)
    tiles(4, 4, lambda k: (1, k + k // 3), free=True)
    tiles(8, 4, lambda k: (2, k + k // 3))
    take_z(2, 0)

    take_v(2, 0)
    send_far("a", 0)
    split_v(vx.at[2, 0], 3, 0)
    take_z(1, 1)
    tiles(12, 3, lambda k: (k, 5))

    take_v(2, 1)
    send_far("a", 1)
    split_v(vx.at[2, 1], 3, 1)
    tiles(15, 3, lambda k: (k, 3))
    take_z(2, 1)
    tiles(18, 3, lambda k: (k, 6))

    mine = lax.rem(y - x + 4, 4)
    mine = jnp.where(mine == 0, 0, jnp.where(mine == 3, 1, jnp.where(mine == 1, 2, 3)))

    def collect(zj, i):
        for half in (None,) if i < 3 else (0, 1):
            for s in range(3):
                wait(yrecv.at[s, zj, i, rows_of(half)], yrecv_sem.at[s, zj, sem_row(i, half)])
        total[zj, i] = (crecv[zj * 4 + mine, i] + yrecv[0, zj, i]) + (yrecv[1, zj, i] + yrecv[2, zj, i])
        if i > 0:
            s = (None, 1, 0, 2)[i]
            remote(total.at[zj, i], xrecv.at[s, zj], osend.at[i - 1, zj], orecv.at[s, zj], at(dx=OFFSET[i]))

    take_a(2, 0)
    for i in (1, 2, 0):
        collect(0, i)
    take_z(3, 0)
    settle(ROWS)
    tiles(0, 7, lambda k: (3, k), half=0, free=True)

    take_a(2, 1)
    for slot in range(7):
        wait(ptile.at[slot, 0, pl.ds(0, HALF)], csend.at[slot])
    tiles(0, 7, lambda k: (3, k), half=1, free=True)
    collect(0, 3)
    take_z(3, 1)
    tiles(7, 1, lambda k: (3, 7), half=1, free=True)
    settle(HALF)
    tiles(0, 1, lambda k: (3, 7), half=0, free=True)
    tiles(1, 3, lambda k: (k, 7), free=True)
    for i in (3, 1, 2, 0):
        collect(1, i)
    wait(ptile.at[0, 0, pl.ds(0, HALF)], csend.at[0])
    for slot in (1, 2, 3):
        wait(ptile.at[slot, 0], csend.at[slot])

    keep = lax.rem(zl + zh, 2)
    for zj in range(2):
        for s in range(3):
            wait(xrecv.at[s, zj], orecv.at[s, zj])

    def summed(zj):
        return (total[zj, 0] + xrecv[0, zj]) + (xrecv[1, zj] + xrecv[2, zj])

    zsend[...] = summed(1 - keep)
    remote(zsend, zrecv, zsem.at[0], zsem.at[1], at(dzh=1))
    result = residual[...] + summed(keep)[: residual.shape[0]]
    wait(zrecv, zsem.at[1])
    out[...] = result + zrecv[: residual.shape[0]]

    wait(zsend, zsem.at[0])
    wait(yrecv, ysend)
    for s in range(3):
        for zj in range(2):
            wait(xrecv.at[s, zj], osend.at[s, zj])
        for half in range(2):
            wait(vx.at[s, half], gsend.at[s, half])
            wait(vx.at[s, half], gsend.at[s, 2 + half])
    for s in range(4):
        for half in range(2):
            wait(vz.at[s, half], fsend.at[s, half])


def body(integrals, amplitudes, residual_in):
    rows, columns = amplitudes.shape
    whole = columns // LANES * LANES
    itg_cols = jnp.pad(integrals[:, whole:], ((0, 0), (0, whole + LANES - columns)))
    amp_cols = jnp.pad(amplitudes[:, whole:], ((0, ROWS - rows), (0, whole + LANES - columns)))
    amp_rows = jnp.pad(amplitudes[ROWS - 8 :], ((0, ROWS - rows), (0, whole + LANES - columns)))
    any_spec = pl.BlockSpec(memory_space=pl.ANY)
    vmem_spec = pl.BlockSpec(memory_space=pltpu.VMEM)
    dma = pltpu.SemaphoreType.DMA
    return pl.pallas_call(
        kernel,
        name="ladder",
        out_shape=jax.ShapeDtypeStruct(residual_in.shape, F32),
        in_specs=[any_spec] * 5 + [vmem_spec],
        out_specs=vmem_spec,
        scratch_shapes=[
            pltpu.VMEM((3, 2, HALF, QUARTER), F32),
            pltpu.VMEM((4, 2, HALF, QUARTER), F32),
            pltpu.VMEM((3, ROWS, QUARTER), F32),
            pltpu.VMEM((2, HALF, QUARTER), F32),
            pltpu.VMEM((8, ROWS, QUARTER), BF16),
            pltpu.VMEM((8, ROWS, QUARTER), BF16),
            pltpu.VMEM((4, ROWS, QUARTER), BF16),
            pltpu.VMEM((4, ROWS, QUARTER), BF16),
            pltpu.VMEM((SLOTS, 2, ROWS, LANES), F32),
            pltpu.VMEM((8, 4, ROWS, LANES), F32),
            pltpu.VMEM((3, 2, 4, ROWS, LANES), F32),
            pltpu.VMEM((3, 2, ROWS, LANES), F32),
            pltpu.VMEM((2, 4, ROWS, LANES), F32),
            pltpu.VMEM((ROWS, LANES), F32),
            pltpu.VMEM((ROWS, LANES), F32),
            dma((2,)),
            dma((3, 4)),
            dma((3, 2)),
            dma((3, 2)),
            dma((4, 2)),
            dma((4, 2)),
            dma((SLOTS,)),
            dma((8, 5)),
            dma,
            dma((3, 2, 5)),
            dma((3, 2)),
            dma((3, 2)),
            dma((2,)),
        ],
        compiler_params=pltpu.CompilerParams(
            collective_id=0, has_side_effects=True, vmem_limit_bytes=60 * 2**20
        ),
        cost_estimate=pl.CostEstimate(flops=3 * 2 * 1008 * 2048 * 2048, bytes_accessed=2 * 2**24, transcendentals=0),
    )(amplitudes, amp_cols, amp_rows, integrals, itg_cols, residual_in)


def solution(mesh):
    return jax.shard_map(
        body,
        mesh=mesh,
        in_specs=(P("occ", "vir"), P("occ", "vir"), P("occ", "vir")),
        out_specs=P("occ", "vir"),
        check_vma=False,
    )
```

```python
import jax
import jax.numpy as jnp
from jax import lax
from jax.experimental import pallas as pl
from jax.experimental.pallas import tpu as pltpu
from jax.sharding import PartitionSpec as P

MESH = pl.DeviceIdType.MESH
F32, BF16 = jnp.float32, jnp.bfloat16

ROWS, HALF, LANES = 256, 128, 128
QUARTER, PART, UNIT, CHUNK = 2048, 1024, 512, 128
SHORT = 16
SLOTS = 8

OFFSET = (0, -1, 1, 2)


def dot(a, b):
    return jnp.dot(a, b, preferred_element_type=F32)


def kernel(
    amp, itg, residual, out, relay_v, relay_a,
    vx, vz, ax, afar, aside, stage_v, stage_a, vhi, vlo, ahi, alo, ptile, crecv, yrecv, xrecv, total, zsend, zrecv,
    own_v, own_a, gsend, grecv_v, grecv_a, hsend_v, hrecv_v, hsend_a, hrecv_a, rsend_v, rsend_a, far_recv, fsend, frecv, csend, crecv_sem, ysend, yrecv_sem,
    osend, orecv, zsem,
):
    occ, vir = lax.axis_index("occ"), lax.axis_index("vir")
    x, zl = lax.rem(occ, 4), occ // 4
    core, y, zh = lax.rem(vir, 2), lax.rem(vir // 2, 4), vir // 8

    def at(dx=0, dzl=0, dy=0, dzh=0, dc=0):
        return (
            lax.rem(zl + dzl, 2) * 4 + lax.rem(x + dx + 4, 4),
            lax.rem(zh + dzh, 2) * 8 + lax.rem(y + dy + 4, 4) * 2 + lax.rem(core + dc, 2),
        )

    peers = [at(dx=1), at(dx=-1), at(dx=2), at(dzl=1), at(dc=1), at(dy=1), at(dy=-1), at(dy=2), at(dzh=1)]
    barrier = pltpu.get_barrier_semaphore()
    for peer in peers:
        pl.semaphore_signal(barrier, inc=1, device_id=peer, device_id_type=MESH)
    pl.semaphore_wait(barrier, len(peers))

    def remote(src, dst, ssem, rsem, device):
        pltpu.make_async_remote_copy(
            src_ref=src, dst_ref=dst, send_sem=ssem, recv_sem=rsem, device_id=device, device_id_type=MESH
        ).start()

    def wait(ref, sem):
        pltpu.make_async_copy(ref, ref, sem).wait()

    def sized(start, size, quarter, act):
        if start + size < QUARTER:
            act(pl.ds(start, size), pl.ds(pl.multiple_of(quarter * QUARTER + start, SHORT), size))
        else:

            @pl.when(quarter != 3)
            def _():
                act(pl.ds(start, size), pl.ds(pl.multiple_of(quarter * QUARTER + start, SHORT), size))

            @pl.when(quarter == 3)
            def _():
                act(pl.ds(start, size - SHORT), pl.ds(3 * QUARTER + start, size - SHORT))

    def quarter_of(dx):
        return lax.rem(x + dx + 4, 4)

    def send(kind, half, dx, s):
        device = at(dx=dx)

        def act(local, whole):
            if kind == "v":
                remote(itg.at[whole], vx.at[s, local], gsend.at[s, half], grecv_v.at[s, half], device)
            else:
                remote(amp.at[whole], ax.at[s, local], gsend.at[s, 2 + half], grecv_a.at[s, half], device)

        sized(half * PART, PART, quarter_of(dx), act)

    def send_near(kind, half):
        send(kind, half, 1, 0)
        send(kind, half, -1, 1)

    def via(way):
        return at(dx=1 - 2 * way)

    def start_v(way):
        def act(local, whole):
            dst = relay_v.at[way, pl.ds(0, local.size)]
            remote(itg.at[whole], dst, hsend_v.at[way], hrecv_v.at[way], via(way))

        sized(way * PART, PART, quarter_of(2), act)

    def pass_v(way):
        def act(local, _):
            src = relay_v.at[way, pl.ds(0, local.size)]
            wait(src, hrecv_v.at[way])
            remote(src, vx.at[2, local], rsend_v.at[way], grecv_v.at[2, way], via(way))

        sized(way * PART, PART, quarter_of(1 - 2 * way), act)

    def start_a(side, way):
        def act(local, whole):
            src = amp.at[whole, pl.ds(0, HALF)] if side == 0 else aside.at[local]
            dst = relay_a.at[side, way, pl.ds(0, local.size)]
            remote(src, dst, hsend_a.at[side, way], hrecv_a.at[side, way], via(way))

        sized(way * PART, PART, quarter_of(2), act)

    def pass_a(side, way):
        def act(local, _):
            src = relay_a.at[side, way, pl.ds(0, local.size)]
            wait(src, hrecv_a.at[side, way])
            remote(src, afar.at[side, local], rsend_a.at[side, way], far_recv.at[side, way], via(way))

        sized(way * PART, PART, quarter_of(1 - 2 * way), act)

    def forward(s, half):
        rows = pl.ds(half * PART, PART)
        remote(vx.at[s, rows], vz.at[s + 1, rows], fsend.at[s + 1, half], frecv.at[s + 1, half], at(dzl=1))

    limit = jnp.where(x == 3, QUARTER - SHORT, QUARTER)

    def known(value, start):
        index = lax.broadcasted_iota(jnp.int32, value.shape, 0) + start
        return jnp.where(index < limit, value, 0.0)

    def split_v(src, j, start, size):
        def step(c, _):
            at_row = pl.multiple_of(c * CHUNK, CHUNK)
            value = known(src[pl.ds(at_row, CHUNK)], start + at_row)
            high = value.astype(BF16)
            rows = pl.ds(pl.multiple_of(start + at_row, CHUNK), CHUNK)
            vhi[j, rows] = high
            vlo[j, rows] = (value - high.astype(F32)).astype(BF16)
            return 0

        lax.fori_loop(0, size // CHUNK, step, 0)

    def split_a(src, i, row0, start, size):
        rows = pl.ds(row0, src.shape[1])

        def step(c, _):
            at_row = pl.multiple_of(c * CHUNK, CHUNK)
            value = known(src[pl.ds(at_row, CHUNK)], start + at_row).T
            high = value.astype(BF16)
            columns = pl.ds(pl.multiple_of(start + at_row, CHUNK), CHUNK)
            ahi[i, rows, columns] = high
            alo[i, rows, columns] = (value - high.astype(F32)).astype(BF16)
            return 0

        lax.fori_loop(0, size // CHUNK, step, 0)

    def take_v(s, half):
        sized(half * PART, PART, x, lambda local, _: wait(vx.at[s, local], grecv_v.at[s, half]))
        forward(s, half)

    def split_taken(s, half):
        split_v(vx.at[s, pl.ds(half * PART, PART)], s + 1, half * PART, PART)

    def take_z(s, half):
        rows = pl.ds(half * PART, PART)
        if s == 0:
            sized(half * PART, PART, x, lambda local, _: wait(vz.at[s, local], frecv.at[s, half]))
        else:
            wait(vz.at[s, rows], frecv.at[s, half])
        split_v(vz.at[s, rows], 4 + s, half * PART, PART)

    def take_a(s, half):
        sized(half * PART, PART, x, lambda local, _: wait(ax.at[s, local], grecv_a.at[s, half]))
        split_a(ax.at[s, pl.ds(half * PART, PART)], s + 1, 0, half * PART, PART)

    def take_far(side):
        for way in range(2):
            sized(way * PART, PART, x, lambda local, _: wait(afar.at[side, local], far_recv.at[side, way]))
        split_a(afar.at[side], 3, side * HALF, 0, QUARTER)

    def load_v(u, act):
        sized(u * UNIT, UNIT, x, lambda local, whole: act(
            itg.at[whole], stage_v.at[u % 2, pl.ds(0, local.size)], own_v.at[u % 2]))

    def load_a(u, act):
        sized(u % 4 * UNIT, UNIT, x if u < 4 else quarter_of(2), lambda local, whole: act(
            amp.at[whole], stage_a.at[u % 2, pl.ds(0, local.size)], own_a.at[u % 2]))

    def begin(src, dst, sem):
        pltpu.make_async_copy(src, dst, sem).start()

    def end(src, dst, sem):
        wait(dst, sem)

    def set_aside(u):
        def step(c, _):
            at_row = pl.multiple_of(c * CHUNK, CHUNK)
            n = amp.shape[1] - HALF
            aside[pl.ds(pl.multiple_of(u % 4 * UNIT + at_row, CHUNK), CHUNK), pl.ds(0, n)] = stage_a[
                u % 2, pl.ds(at_row, CHUNK), pl.ds(HALF, n)
            ]
            return 0

        lax.fori_loop(0, UNIT // CHUNK, step, 0)

    def rows_of(half):
        return pl.ds(0, ROWS) if half is None else pl.ds(half * HALF, HALF)

    def sem_row(i, half):
        return i if half is None else 3 + half

    def produce(i, j, half, slot, free):
        rows = rows_of(half)
        n = ROWS if half is None else HALF
        if not free:
            wait(ptile.at[slot, 0, pl.ds(0, n)], csend.at[slot])
        high, low = ahi[i, rows], alo[i, rows]
        both = jnp.concatenate([high, low], axis=0)
        one = dot(both, vhi[j])
        if half is None:
            value = one[:n] + one[n:] + dot(high, vlo[j])
        else:
            two = dot(both, vlo[j])
            value = one[:n] + one[n:] + two[:n] + two[n:]
        ptile[slot, 0, pl.ds(0, n)] = value[:, :LANES]
        ptile[slot, 1, pl.ds(0, n)] = value[:, LANES:]
        remote(
            ptile.at[slot, 1 - core, pl.ds(0, n)], crecv.at[j, i, rows],
            csend.at[slot], crecv_sem.at[j, sem_row(i, half)], at(dc=1),
        )

    def finish(i, j, half, slot):
        rows = rows_of(half)
        n = ROWS if half is None else HALF
        wait(crecv.at[j, i, rows], crecv_sem.at[j, sem_row(i, half)])
        crecv[j, i, rows] += ptile[slot, core, pl.ds(0, n)]
        d, zj = lax.rem(j, 4), j // 4
        shift = jnp.where(d == 0, 4, jnp.where(d == 1, 3, jnp.where(d == 2, 5, 6)))
        target = lax.rem(x + shift, 4)
        distance = lax.rem(y - target + 4, 4)

        @pl.when(distance != 0)
        def _():
            remote(
                crecv.at[j, i, rows], yrecv.at[distance - 1, zj, i, rows],
                ysend, yrecv_sem.at[distance - 1, zj, sem_row(i, half)],
                (occ, zh * 8 + target * 2 + core),
            )

    def tiles(count, n, index, half=None, free=False):
        def step(k, _):
            @pl.when(k < n)
            def _():
                i, j = index(k)
                produce(i, j, half, lax.rem(count + k, SLOTS), free)

            @pl.when(k > 0)
            def _():
                i, j = index(k - 1)
                finish(i, j, half, lax.rem(count + k - 1, SLOTS))

            return 0

        lax.fori_loop(0, n + 1, step, 0)

    def settle(n):
        for slot in range(SLOTS):
            wait(ptile.at[slot, 0, pl.ds(0, n)], csend.at[slot])

    for half in range(2):
        send_near("v", half)
        sized(half * PART, PART, x, lambda local, whole, half=half: remote(
            itg.at[whole], vz.at[0, local], fsend.at[0, half], frecv.at[0, half], at(dzl=1)))
    send_near("a", 0)
    for way in range(2):
        start_v(way)
    send_near("a", 1)
    for u in range(2):
        load_v(u, begin)
        load_a(u, begin)
    for u in range(4):
        load_v(u, end)
        split_v(stage_v.at[u % 2], 0, u * UNIT, UNIT)
        if u < 2:
            load_v(u + 2, begin)
    for u in range(8):
        load_a(u, end)
        if u < 4:
            split_a(stage_a.at[u % 2], 0, 0, u * UNIT, UNIT)
        else:
            set_aside(u)
        if u < 6:
            load_a(u + 2, begin)

    take_v(0, 0)
    take_v(1, 0)
    split_taken(0, 0)
    split_taken(1, 0)
    take_z(0, 0)

    take_v(0, 1)
    take_v(1, 1)
    split_taken(0, 1)
    split_taken(1, 1)
    take_z(0, 1)
    tiles(0, 4, lambda k: (0, k + k // 3), free=True)

    take_a(0, 0)
    take_a(1, 0)
    take_z(1, 0)

    for way in range(2):
        pass_v(way)
    for side in range(2):
        for way in range(2):
            start_a(side, way)
    take_z(2, 0)

    take_a(0, 1)
    take_a(1, 1)
    tiles(4, 4, lambda k: (1, k + k // 3), free=True)
    tiles(8, 4, lambda k: (2, k + k // 3))
    take_z(1, 1)
    tiles(12, 3, lambda k: (k, 5))

    take_v(2, 0)
    take_v(2, 1)
    split_taken(2, 0)
    split_taken(2, 1)
    tiles(15, 3, lambda k: (k, 3))
    take_z(2, 1)
    tiles(18, 3, lambda k: (k, 6))

    mine = lax.rem(y - x + 4, 4)
    mine = jnp.where(mine == 0, 0, jnp.where(mine == 3, 1, jnp.where(mine == 1, 2, 3)))

    def collect(zj, i):
        for half in (None,) if i < 3 else (0, 1):
            for s in range(3):
                wait(yrecv.at[s, zj, i, rows_of(half)], yrecv_sem.at[s, zj, sem_row(i, half)])
        total[zj, i] = (crecv[zj * 4 + mine, i] + yrecv[0, zj, i]) + (yrecv[1, zj, i] + yrecv[2, zj, i])
        if i > 0:
            s = (None, 1, 0, 2)[i]
            remote(total.at[zj, i], xrecv.at[s, zj], osend.at[i - 1, zj], orecv.at[s, zj], at(dx=OFFSET[i]))

    for way in range(2):
        pass_a(0, way)
    for i in (1, 2, 0):
        collect(0, i)
    for way in range(2):
        pass_a(1, way)
    take_z(3, 0)
    take_far(0)
    settle(ROWS)
    tiles(0, 7, lambda k: (3, k), half=0, free=True)

    take_far(1)
    for slot in range(7):
        wait(ptile.at[slot, 0, pl.ds(0, HALF)], csend.at[slot])
    tiles(0, 7, lambda k: (3, k), half=1, free=True)
    collect(0, 3)
    take_z(3, 1)
    tiles(7, 1, lambda k: (3, 7), half=1, free=True)
    settle(HALF)
    tiles(0, 1, lambda k: (3, 7), half=0, free=True)
    tiles(1, 3, lambda k: (k, 7), free=True)
    for i in (3, 1, 2, 0):
        collect(1, i)
    wait(ptile.at[0, 0, pl.ds(0, HALF)], csend.at[0])
    for slot in (1, 2, 3):
        wait(ptile.at[slot, 0], csend.at[slot])

    keep = lax.rem(zl + zh, 2)
    for zj in range(2):
        for s in range(3):
            wait(xrecv.at[s, zj], orecv.at[s, zj])

    def summed(zj):
        return (total[zj, 0] + xrecv[0, zj]) + (xrecv[1, zj] + xrecv[2, zj])

    zsend[...] = summed(1 - keep)
    remote(zsend, zrecv, zsem.at[0], zsem.at[1], at(dzh=1))
    result = residual[...] + summed(keep)[: residual.shape[0]]
    wait(zrecv, zsem.at[1])
    out[...] = result + zrecv[: residual.shape[0]]

    wait(zsend, zsem.at[0])
    wait(yrecv, ysend)
    for s in range(3):
        for zj in range(2):
            wait(xrecv.at[s, zj], osend.at[s, zj])
    for half in range(2):
        for s, dx in enumerate((1, -1)):
            sized(half * PART, PART, quarter_of(dx), lambda local, _: wait(vx.at[s, local], gsend.at[s, half]))
            sized(half * PART, PART, quarter_of(dx), lambda local, _: wait(ax.at[s, local], gsend.at[s, 2 + half]))
        way = half
        sized(way * PART, PART, quarter_of(2), lambda local, _: wait(vx.at[2, local], hsend_v.at[way]))
        sized(way * PART, PART, quarter_of(1 - 2 * way), lambda local, _: wait(vx.at[2, local], rsend_v.at[way]))
        for side in range(2):
            sized(way * PART, PART, quarter_of(2), lambda local, _: wait(afar.at[side, local], hsend_a.at[side, way]))
            sized(way * PART, PART, quarter_of(1 - 2 * way), lambda local, _: wait(afar.at[side, local], rsend_a.at[side, way]))
    for half in range(2):
        sized(half * PART, PART, x, lambda local, _: wait(vz.at[0, local], fsend.at[0, half]))
        for s in range(1, 4):
            wait(vz.at[s, pl.ds(half * PART, PART)], fsend.at[s, half])


def body(integrals, amplitudes, residual_in):
    rows = amplitudes.shape[0]
    any_spec = pl.BlockSpec(memory_space=pl.ANY)
    vmem_spec = pl.BlockSpec(memory_space=pltpu.VMEM)
    dma = pltpu.SemaphoreType.DMA
    return pl.pallas_call(
        kernel,
        name="ladder",
        out_shape=(
            jax.ShapeDtypeStruct(residual_in.shape, F32),
            jax.ShapeDtypeStruct((2, PART, ROWS), F32),
            jax.ShapeDtypeStruct((2, 2, PART, HALF), F32),
        ),
        in_specs=[any_spec] * 2 + [vmem_spec],
        out_specs=(vmem_spec, any_spec, any_spec),
        scratch_shapes=[
            pltpu.VMEM((3, QUARTER, ROWS), F32),
            pltpu.VMEM((4, QUARTER, ROWS), F32),
            pltpu.VMEM((2, QUARTER, rows), F32),
            pltpu.VMEM((2, QUARTER, HALF), F32),
            pltpu.VMEM((QUARTER, HALF), F32),
            pltpu.VMEM((2, UNIT, ROWS), F32),
            pltpu.VMEM((2, UNIT, rows), F32),
            pltpu.VMEM((8, QUARTER, ROWS), BF16),
            pltpu.VMEM((8, QUARTER, ROWS), BF16),
            pltpu.VMEM((4, ROWS, QUARTER), BF16),
            pltpu.VMEM((4, ROWS, QUARTER), BF16),
            pltpu.VMEM((SLOTS, 2, ROWS, LANES), F32),
            pltpu.VMEM((8, 4, ROWS, LANES), F32),
            pltpu.VMEM((3, 2, 4, ROWS, LANES), F32),
            pltpu.VMEM((3, 2, ROWS, LANES), F32),
            pltpu.VMEM((2, 4, ROWS, LANES), F32),
            pltpu.VMEM((ROWS, LANES), F32),
            pltpu.VMEM((ROWS, LANES), F32),
            dma((2,)),
            dma((2,)),
            dma((2, 4)),
            dma((3, 2)),
            dma((2, 2)),
            dma((2,)),
            dma((2,)),
            dma((2, 2)),
            dma((2, 2)),
            dma((2,)),
            dma((2, 2)),
            dma((2, 2)),
            dma((4, 2)),
            dma((4, 2)),
            dma((SLOTS,)),
            dma((8, 5)),
            dma,
            dma((3, 2, 5)),
            dma((3, 2)),
            dma((3, 2)),
            dma((2,)),
        ],
        compiler_params=pltpu.CompilerParams(
            collective_id=0, has_side_effects=True, vmem_limit_bytes=61 * 2**20
        ),
        cost_estimate=pl.CostEstimate(flops=3 * 2 * 1008 * 2048 * 2048, bytes_accessed=2 * 2**24, transcendentals=0),
    )(amplitudes.T, integrals.T, residual_in)[0]


def solution(mesh):
    return jax.shard_map(
        body,
        mesh=mesh,
        in_specs=(P("occ", "vir"), P("occ", "vir"), P("occ", "vir")),
        out_specs=P("occ", "vir"),
        check_vma=False,
    )
```

```python
import jax
import jax.numpy as jnp
from jax import lax
from jax.experimental import pallas as pl
from jax.experimental.pallas import tpu as pltpu
from jax.sharding import PartitionSpec as P

MESH = pl.DeviceIdType.MESH
F32, BF16 = jnp.float32, jnp.bfloat16

ROWS, HALF, LANES = 256, 128, 128
QUARTER, PART, UNIT, CHUNK = 2048, 1024, 512, 128
SHORT = 16
SLOTS = 4

OFFSET = (0, -1, 1, 2)


def dot(a, b):
    return jnp.dot(a, b, preferred_element_type=F32)


def kernel(
    amp, itg, out, relay_v, relay_a,
    vx, vz, ax, afar, aside, stage_v, stage_a, vhi, vlo, ahi, alo, ptile, plast, crecv, yrecv, xrecv, total, zsend, zrecv,
    own_v, own_a, gsend, grecv_v, grecv_a, hsend_v, hrecv_v, hsend_a, hrecv_a, rsend_v, rsend_a, far_recv, fsend, frecv, csend, lsend, crecv_sem, ysend, yrecv_sem,
    osend, orecv, zsem,
):
    occ, vir = lax.axis_index("occ"), lax.axis_index("vir")
    x, zl = lax.rem(occ, 4), occ // 4
    core, y, zh = lax.rem(vir, 2), lax.rem(vir // 2, 4), vir // 8

    def at(dx=0, dzl=0, dy=0, dzh=0, dc=0):
        return (
            lax.rem(zl + dzl, 2) * 4 + lax.rem(x + dx + 4, 4),
            lax.rem(zh + dzh, 2) * 8 + lax.rem(y + dy + 4, 4) * 2 + lax.rem(core + dc, 2),
        )

    peers = [at(dx=1), at(dx=-1), at(dx=2), at(dzl=1), at(dc=1), at(dy=1), at(dy=-1), at(dy=2), at(dzh=1)]
    barrier = pltpu.get_barrier_semaphore()
    for peer in peers:
        pl.semaphore_signal(barrier, inc=1, device_id=peer, device_id_type=MESH)
    pl.semaphore_wait(barrier, len(peers))

    def remote(src, dst, ssem, rsem, device):
        pltpu.make_async_remote_copy(
            src_ref=src, dst_ref=dst, send_sem=ssem, recv_sem=rsem, device_id=device, device_id_type=MESH
        ).start()

    def wait(ref, sem):
        pltpu.make_async_copy(ref, ref, sem).wait()

    def sized(start, size, quarter, act):
        if start + size < QUARTER:
            act(pl.ds(start, size), pl.ds(pl.multiple_of(quarter * QUARTER + start, SHORT), size))
        else:

            @pl.when(quarter != 3)
            def _():
                act(pl.ds(start, size), pl.ds(pl.multiple_of(quarter * QUARTER + start, SHORT), size))

            @pl.when(quarter == 3)
            def _():
                act(pl.ds(start, size - SHORT), pl.ds(3 * QUARTER + start, size - SHORT))

    def quarter_of(dx):
        return lax.rem(x + dx + 4, 4)

    def send(kind, half, dx, s):
        device = at(dx=dx)

        def act(local, whole):
            if kind == "v":
                remote(itg.at[whole], vx.at[s, local], gsend.at[s, half], grecv_v.at[s, half], device)
            else:
                remote(amp.at[whole], ax.at[s, local], gsend.at[s, 2 + half], grecv_a.at[s, half], device)

        sized(half * PART, PART, quarter_of(dx), act)

    def send_near(kind, half):
        send(kind, half, 1, 0)
        send(kind, half, -1, 1)

    def via(way):
        return at(dx=1 - 2 * way)

    def start_v(way):
        def act(local, whole):
            dst = relay_v.at[way, pl.ds(0, local.size)]
            remote(itg.at[whole], dst, hsend_v.at[way], hrecv_v.at[way], via(way))

        sized(way * PART, PART, quarter_of(2), act)

    def pass_v(way):
        def act(local, _):
            src = relay_v.at[way, pl.ds(0, local.size)]
            wait(src, hrecv_v.at[way])
            remote(src, vx.at[2, local], rsend_v.at[way], grecv_v.at[2, way], via(way))

        sized(way * PART, PART, quarter_of(1 - 2 * way), act)

    def start_a(side, way):
        def act(local, whole):
            src = amp.at[whole, pl.ds(0, HALF)] if side == 0 else aside.at[local]
            dst = relay_a.at[side, way, pl.ds(0, local.size)]
            remote(src, dst, hsend_a.at[side, way], hrecv_a.at[side, way], via(way))

        sized(way * PART, PART, quarter_of(2), act)

    def pass_a(side, way):
        def act(local, _):
            src = relay_a.at[side, way, pl.ds(0, local.size)]
            wait(src, hrecv_a.at[side, way])
            remote(src, afar.at[side, local], rsend_a.at[side, way], far_recv.at[side, way], via(way))

        sized(way * PART, PART, quarter_of(1 - 2 * way), act)

    def forward(s, half):
        rows = pl.ds(half * PART, PART)
        remote(vx.at[s, rows], vz.at[s + 1, rows], fsend.at[s + 1, half], frecv.at[s + 1, half], at(dzl=1))

    limit = jnp.where(x == 3, QUARTER - SHORT, QUARTER)

    def known(value, start):
        index = lax.broadcasted_iota(jnp.int32, value.shape, 0) + start
        return jnp.where(index < limit, value, 0.0)

    def split_v(src, j, start, size, lanes=pl.ds(0, ROWS)):
        def step(c, _):
            at_row = pl.multiple_of(c * CHUNK, CHUNK)
            value = known(src[pl.ds(at_row, CHUNK)], start + at_row)
            high = value.astype(BF16)
            rows = pl.ds(pl.multiple_of(start + at_row, CHUNK), CHUNK)
            vhi[j, rows, lanes] = high
            vlo[j, rows, lanes] = (value - high.astype(F32)).astype(BF16)
            return 0

        lax.fori_loop(0, size // CHUNK, step, 0)

    def split_a(src, i, row0, start, size):
        rows = pl.ds(row0, src.shape[1])

        def step(c, _):
            at_row = pl.multiple_of(c * CHUNK, CHUNK)
            value = known(src[pl.ds(at_row, CHUNK)], start + at_row).T
            high = value.astype(BF16)
            columns = pl.ds(pl.multiple_of(start + at_row, CHUNK), CHUNK)
            ahi[i, rows, columns] = high
            alo[i, rows, columns] = (value - high.astype(F32)).astype(BF16)
            return 0

        lax.fori_loop(0, size // CHUNK, step, 0)

    def take_v(s, half):
        sized(half * PART, PART, x, lambda local, _: wait(vx.at[s, local], grecv_v.at[s, half]))
        if s < 2:
            forward(s, half)

    def forward_last(side):
        lanes = pl.ds(side * LANES, LANES)
        remote(vx.at[2, :, lanes], vz.at[3, :, lanes], fsend.at[3, side], frecv.at[3, side], at(dzl=1))

    def take_last(side):
        lanes = pl.ds(side * LANES, LANES)
        wait(vz.at[3, :, lanes], frecv.at[3, side])
        split_v(vz.at[3, :, lanes], 7, 0, QUARTER, lanes)

    def split_taken(s, half):
        split_v(vx.at[s, pl.ds(half * PART, PART)], s + 1, half * PART, PART)

    def take_z(s, half):
        rows = pl.ds(half * PART, PART)
        if s == 0:
            sized(half * PART, PART, x, lambda local, _: wait(vz.at[s, local], frecv.at[s, half]))
        else:
            wait(vz.at[s, rows], frecv.at[s, half])
        split_v(vz.at[s, rows], 4 + s, half * PART, PART)

    def take_a(s, half):
        sized(half * PART, PART, x, lambda local, _: wait(ax.at[s, local], grecv_a.at[s, half]))
        split_a(ax.at[s, pl.ds(half * PART, PART)], s + 1, 0, half * PART, PART)

    def take_far(side):
        for way in range(2):
            sized(way * PART, PART, x, lambda local, _: wait(afar.at[side, local], far_recv.at[side, way]))
        split_a(afar.at[side], 3, side * HALF, 0, QUARTER)

    def load_v(u, act):
        sized(u * UNIT, UNIT, x, lambda local, whole: act(
            itg.at[whole], stage_v.at[u % 2, pl.ds(0, local.size)], own_v.at[u % 2]))

    def load_a(u, act):
        sized(u % 4 * UNIT, UNIT, x if u < 4 else quarter_of(2), lambda local, whole: act(
            amp.at[whole], stage_a.at[u % 2, pl.ds(0, local.size)], own_a.at[u % 2]))

    def begin(src, dst, sem):
        pltpu.make_async_copy(src, dst, sem).start()

    def end(src, dst, sem):
        wait(dst, sem)

    def set_aside(u):
        def step(c, _):
            at_row = pl.multiple_of(c * CHUNK, CHUNK)
            n = amp.shape[1] - HALF
            aside[pl.ds(pl.multiple_of(u % 4 * UNIT + at_row, CHUNK), CHUNK), pl.ds(0, n)] = stage_a[
                u % 2, pl.ds(at_row, CHUNK), pl.ds(HALF, n)
            ]
            return 0

        lax.fori_loop(0, UNIT // CHUNK, step, 0)

    def rows_of(half):
        return pl.ds(0, ROWS) if half is None else pl.ds(half * HALF, HALF)

    def sem_row(i, half):
        return i if half is None else 3 + half

    def product(i, rows, n, high_v, low_v):
        high, low = ahi[i, rows], alo[i, rows]
        both = jnp.concatenate([high, low], axis=0)
        one = dot(both, high_v)
        if n == ROWS:
            return one[:n] + one[n:] + dot(high, low_v)
        two = dot(both, low_v)
        return one[:n] + one[n:] + two[:n] + two[n:]

    def produce(i, j, half, slot):
        rows = rows_of(half)
        n = ROWS if half is None else HALF
        value = product(i, rows, n, vhi[j], vlo[j])
        ptile[slot, 0, pl.ds(0, n)] = value[:, :LANES]
        ptile[slot, 1, pl.ds(0, n)] = value[:, LANES:]
        remote(
            ptile.at[slot, 1 - core, pl.ds(0, n)], crecv.at[j, i, rows],
            csend.at[slot], crecv_sem.at[j, sem_row(i, half)], at(dc=1),
        )

    def finish(i, j, half, own):
        rows = rows_of(half)
        n = ROWS if half is None else HALF
        wait(crecv.at[j, i, rows], crecv_sem.at[j, sem_row(i, half)])
        crecv[j, i, rows] += own[pl.ds(0, n)]
        d, zj = lax.rem(j, 4), j // 4
        shift = jnp.where(d == 0, 4, jnp.where(d == 1, 3, jnp.where(d == 2, 5, 6)))
        target = lax.rem(x + shift, 4)
        distance = lax.rem(y - target + 4, 4)

        @pl.when(distance != 0)
        def _():
            remote(
                crecv.at[j, i, rows], yrecv.at[distance - 1, zj, i, rows],
                ysend, yrecv_sem.at[distance - 1, zj, sem_row(i, half)],
                (occ, zh * 8 + target * 2 + core),
            )

    def tiles(count, n, index, half=None, free=0):
        def step(k, _):
            @pl.when(k < n)
            def _():
                i, j = index(k)
                slot = lax.rem(count + k, SLOTS)

                @pl.when(k >= free)
                def _():
                    wait(ptile.at[slot, 0, pl.ds(0, ROWS if half is None else HALF)], csend.at[slot])

                produce(i, j, half, slot)

            @pl.when(k > 0)
            def _():
                i, j = index(k - 1)
                finish(i, j, half, ptile.at[lax.rem(count + k - 1, SLOTS), core])

            return 0

        lax.fori_loop(0, n + 1, step, 0)

    def settle(n):
        for slot in range(SLOTS):
            wait(ptile.at[slot, 0, pl.ds(0, n)], csend.at[slot])

    def last_tiles(side, n, half=None):
        lanes = pl.ds(side * LANES, LANES)
        rows = rows_of(half)
        block = (lambda k: k) if half is None else (lambda k: 3)

        def step(k, _):
            @pl.when(k < n)
            def _():
                i = block(k)
                plast[side, i, rows] = product(i, rows, ROWS if half is None else HALF, vhi[7, :, lanes], vlo[7, :, lanes])

                @pl.when(core != side)
                def _():
                    remote(
                        plast.at[side, i, rows], crecv.at[7, i, rows],
                        lsend.at[side, sem_row(i, half)], crecv_sem.at[7, sem_row(i, half)], at(dc=1),
                    )

            @pl.when((k > 0) & (core == side))
            def _():
                i = block(k - 1)
                finish(i, 7, half, plast.at[side, i, rows])

            return 0

        lax.fori_loop(0, n + 1, step, 0)

    for half in range(2):
        send_near("v", half)
        sized(half * PART, PART, x, lambda local, whole, half=half: remote(
            itg.at[whole], vz.at[0, local], fsend.at[0, half], frecv.at[0, half], at(dzl=1)))
    send_near("a", 0)
    for way in range(2):
        start_v(way)
    send_near("a", 1)
    for u in range(2):
        load_v(u, begin)
        load_a(u, begin)
    for u in range(4):
        load_v(u, end)
        split_v(stage_v.at[u % 2], 0, u * UNIT, UNIT)
        if u < 2:
            load_v(u + 2, begin)
    for u in range(8):
        load_a(u, end)
        if u < 4:
            split_a(stage_a.at[u % 2], 0, 0, u * UNIT, UNIT)
        else:
            set_aside(u)
        if u < 6:
            load_a(u + 2, begin)

    take_v(0, 0)
    take_v(1, 0)
    split_taken(0, 0)
    split_taken(1, 0)
    take_z(0, 0)

    take_v(0, 1)
    take_v(1, 1)
    split_taken(0, 1)
    split_taken(1, 1)
    take_z(0, 1)
    tiles(0, 4, lambda k: (0, k + k // 3), free=4)

    take_a(0, 0)
    take_a(1, 0)
    take_z(1, 0)

    for way in range(2):
        pass_v(way)
    for side in range(2):
        for way in range(2):
            start_a(side, way)
    take_z(2, 0)

    take_a(0, 1)
    take_a(1, 1)
    tiles(4, 8, lambda k: (1 + k // 4, k % 4 + k % 4 // 3))
    take_z(1, 1)
    tiles(12, 3, lambda k: (k, 5))

    take_v(2, 0)
    take_v(2, 1)
    forward_last(0)
    forward_last(1)
    split_taken(2, 0)
    split_taken(2, 1)
    tiles(15, 3, lambda k: (k, 3))
    take_z(2, 1)
    tiles(18, 3, lambda k: (k, 6))

    mine = lax.rem(y - x + 4, 4)
    mine = jnp.where(mine == 0, 0, jnp.where(mine == 3, 1, jnp.where(mine == 1, 2, 3)))

    def collect(zj, i, half=None):
        row = sem_row(i, half)
        start = 0 if half is None else half * HALF
        for s in range(3):
            wait(yrecv.at[s, zj, i, rows_of(half)], yrecv_sem.at[s, zj, row])

        def step(c, _):
            rows = pl.ds(pl.multiple_of(start + c * 32, 32), 32)
            total[zj, i, rows] = (crecv[zj * 4 + mine, i, rows] + yrecv[0, zj, i, rows]) + (
                yrecv[1, zj, i, rows] + yrecv[2, zj, i, rows]
            )
            return 0

        lax.fori_loop(0, (ROWS if half is None else HALF) // 32, step, 0)
        if i > 0:
            s, rows = (None, 1, 0, 2)[i], rows_of(half)
            remote(
                total.at[zj, i, rows], xrecv.at[s, zj, rows],
                osend.at[row - 1, zj], orecv.at[row - 1, zj], at(dx=OFFSET[i]),
            )

    late = mine == 3

    for way in range(2):
        pass_a(0, way)
    for i in (1, 2, 0):
        collect(0, i)

    @pl.when(~late)
    def _():
        for i in (1, 2, 0):
            collect(1, i)

    for way in range(2):
        pass_a(1, way)
    take_last(0)
    last_tiles(0, 3)
    take_far(0)
    settle(ROWS)
    tiles(0, 7, lambda k: (3, k), half=0, free=SLOTS)
    last_tiles(0, 1, half=0)
    collect(0, 3, 0)

    @pl.when(~late)
    def _():
        collect(1, 3, 0)

    @pl.when(late & (core == 0))
    def _():
        for i in (1, 2, 0):
            collect(1, i)
        collect(1, 3, 0)

    settle(HALF)
    take_last(1)
    last_tiles(1, 3)
    last_tiles(1, 1, half=0)
    take_far(1)
    tiles(0, 7, lambda k: (3, k), half=1, free=SLOTS)
    last_tiles(0, 1, half=1)
    last_tiles(1, 1, half=1)

    @pl.when(late & (core == 1))
    def _():
        for i in (1, 2, 0):
            collect(1, i)
        collect(1, 3, 0)

    collect(0, 3, 1)
    collect(1, 3, 1)

    keep = lax.rem(zl + zh, 2)
    parts = [(i, None) for i in (1, 2)] + [(3, half) for half in range(2)]
    for zj in range(2):
        for i, half in parts:
            wait(xrecv.at[(None, 1, 0, 2)[i], zj, rows_of(half)], orecv.at[sem_row(i, half) - 1, zj])

    def summed(zj):
        return (total[zj, 0] + xrecv[0, zj]) + (xrecv[1, zj] + xrecv[2, zj])

    zsend[...] = summed(1 - keep)
    remote(zsend, zrecv, zsem.at[0], zsem.at[1], at(dzh=1))
    result = summed(keep)[: out.shape[0]]
    wait(zrecv, zsem.at[1])
    out[...] = result + zrecv[: out.shape[0]]

    wait(zsend, zsem.at[0])
    wait(yrecv, ysend)
    settle(HALF)
    for zj in range(2):
        for i, half in parts:
            wait(total.at[zj, i, rows_of(half)], osend.at[sem_row(i, half) - 1, zj])
    for side in range(2):

        @pl.when(core != side)
        def _():
            for i, half in [(0, None)] + parts:
                wait(plast.at[side, i, rows_of(half)], lsend.at[side, sem_row(i, half)])

    for half in range(2):
        for s, dx in enumerate((1, -1)):
            sized(half * PART, PART, quarter_of(dx), lambda local, _: wait(vx.at[s, local], gsend.at[s, half]))
            sized(half * PART, PART, quarter_of(dx), lambda local, _: wait(ax.at[s, local], gsend.at[s, 2 + half]))
        way = half
        sized(way * PART, PART, quarter_of(2), lambda local, _: wait(vx.at[2, local], hsend_v.at[way]))
        sized(way * PART, PART, quarter_of(1 - 2 * way), lambda local, _: wait(vx.at[2, local], rsend_v.at[way]))
        for side in range(2):
            sized(way * PART, PART, quarter_of(2), lambda local, _: wait(afar.at[side, local], hsend_a.at[side, way]))
            sized(way * PART, PART, quarter_of(1 - 2 * way), lambda local, _: wait(afar.at[side, local], rsend_a.at[side, way]))
    for half in range(2):
        sized(half * PART, PART, x, lambda local, _: wait(vz.at[0, local], fsend.at[0, half]))
        for s in range(1, 4):
            wait(vz.at[s, pl.ds(half * PART, PART)], fsend.at[s, half])


def body(integrals, amplitudes, residual_in):
    rows = amplitudes.shape[0]
    any_spec = pl.BlockSpec(memory_space=pl.ANY)
    vmem_spec = pl.BlockSpec(memory_space=pltpu.VMEM)
    dma = pltpu.SemaphoreType.DMA
    ladder = pl.pallas_call(
        kernel,
        name="ladder",
        out_shape=(
            jax.ShapeDtypeStruct(residual_in.shape, F32),
            jax.ShapeDtypeStruct((2, PART, ROWS), F32),
            jax.ShapeDtypeStruct((2, 2, PART, HALF), F32),
        ),
        in_specs=[any_spec] * 2,
        out_specs=(vmem_spec, any_spec, any_spec),
        scratch_shapes=[
            pltpu.VMEM((3, QUARTER, ROWS), F32),
            pltpu.VMEM((4, QUARTER, ROWS), F32),
            pltpu.VMEM((2, QUARTER, rows), F32),
            pltpu.VMEM((2, QUARTER, HALF), F32),
            pltpu.VMEM((QUARTER, HALF), F32),
            pltpu.VMEM((2, UNIT, ROWS), F32),
            pltpu.VMEM((2, UNIT, rows), F32),
            pltpu.VMEM((8, QUARTER, ROWS), BF16),
            pltpu.VMEM((8, QUARTER, ROWS), BF16),
            pltpu.VMEM((4, ROWS, QUARTER), BF16),
            pltpu.VMEM((4, ROWS, QUARTER), BF16),
            pltpu.VMEM((SLOTS, 2, ROWS, LANES), F32),
            pltpu.VMEM((2, 4, ROWS, LANES), F32),
            pltpu.VMEM((8, 4, ROWS, LANES), F32),
            pltpu.VMEM((3, 2, 4, ROWS, LANES), F32),
            pltpu.VMEM((3, 2, ROWS, LANES), F32),
            pltpu.VMEM((2, 4, ROWS, LANES), F32),
            pltpu.VMEM((ROWS, LANES), F32),
            pltpu.VMEM((ROWS, LANES), F32),
            dma((2,)),
            dma((2,)),
            dma((2, 4)),
            dma((3, 2)),
            dma((2, 2)),
            dma((2,)),
            dma((2,)),
            dma((2, 2)),
            dma((2, 2)),
            dma((2,)),
            dma((2, 2)),
            dma((2, 2)),
            dma((4, 2)),
            dma((4, 2)),
            dma((SLOTS,)),
            dma((2, 5)),
            dma((8, 5)),
            dma,
            dma((3, 2, 5)),
            dma((4, 2)),
            dma((4, 2)),
            dma((2,)),
        ],
        compiler_params=pltpu.CompilerParams(
            collective_id=0, has_side_effects=True, vmem_limit_bytes=61 * 2**20
        ),
        cost_estimate=pl.CostEstimate(flops=3 * 2 * 1008 * 2048 * 2048, bytes_accessed=2 * 2**24, transcendentals=0),
    )(amplitudes.T, integrals.T)[0]
    return residual_in + ladder


def solution(mesh):
    return jax.shard_map(
        body,
        mesh=mesh,
        in_specs=(P("occ", "vir"), P("occ", "vir"), P("occ", "vir")),
        out_specs=P("occ", "vir"),
        check_vma=False,
    )
```

```python
import jax
import jax.numpy as jnp
from jax import lax
from jax.experimental import pallas as pl
from jax.experimental.pallas import tpu as pltpu
from jax.sharding import PartitionSpec as P

MESH = pl.DeviceIdType.MESH
F32, BF16 = jnp.float32, jnp.bfloat16

ROWS, HALF, LANES = 256, 128, 128
QUARTER, PART, UNIT, CHUNK = 2048, 1024, 512, 128
SHORT = 16
SLOTS = 4

OFFSET = (0, -1, 1, 2)


def dot(a, b):
    return jnp.dot(a, b, preferred_element_type=F32)


def kernel(
    amp, itg, out, relay_v, relay_a,
    vx, vz, ax, afar, aside, stage_v, stage_a, vhi, vlo, ahi, alo, ptile, plast, crecv, yrecv, xrecv, total, zsend, zrecv,
    own_v, own_a, gsend, grecv_v, grecv_a, hsend_v, hrecv_v, hsend_a, hrecv_a, rsend_v, rsend_a, far_recv, fsend, frecv, csend, lsend, crecv_sem, ysend, yrecv_sem,
    osend, orecv, zsem,
):
    occ, vir = lax.axis_index("occ"), lax.axis_index("vir")
    x, zl = lax.rem(occ, 4), occ // 4
    core, y, zh = lax.rem(vir, 2), lax.rem(vir // 2, 4), vir // 8

    def at(dx=0, dzl=0, dy=0, dzh=0, dc=0):
        return (
            lax.rem(zl + dzl, 2) * 4 + lax.rem(x + dx + 4, 4),
            lax.rem(zh + dzh, 2) * 8 + lax.rem(y + dy + 4, 4) * 2 + lax.rem(core + dc, 2),
        )

    peers = [at(dx=1), at(dx=-1), at(dx=2), at(dzl=1), at(dc=1), at(dy=1), at(dy=-1), at(dy=2), at(dzh=1)]
    barrier = pltpu.get_barrier_semaphore()
    for peer in peers:
        pl.semaphore_signal(barrier, inc=1, device_id=peer, device_id_type=MESH)
    pl.semaphore_wait(barrier, len(peers))

    def remote(src, dst, ssem, rsem, device):
        pltpu.make_async_remote_copy(
            src_ref=src, dst_ref=dst, send_sem=ssem, recv_sem=rsem, device_id=device, device_id_type=MESH
        ).start()

    def wait(ref, sem):
        pltpu.make_async_copy(ref, ref, sem).wait()

    def sized(start, size, quarter, act):
        if start + size < QUARTER:
            act(pl.ds(start, size), pl.ds(pl.multiple_of(quarter * QUARTER + start, SHORT), size))
        else:

            @pl.when(quarter != 3)
            def _():
                act(pl.ds(start, size), pl.ds(pl.multiple_of(quarter * QUARTER + start, SHORT), size))

            @pl.when(quarter == 3)
            def _():
                act(pl.ds(start, size - SHORT), pl.ds(3 * QUARTER + start, size - SHORT))

    def quarter_of(dx):
        return lax.rem(x + dx + 4, 4)

    def send(kind, half, dx, s):
        device = at(dx=dx)

        def act(local, whole):
            if kind == "v":
                remote(itg.at[whole], vx.at[s, local], gsend.at[s, half], grecv_v.at[s, half], device)
            else:
                remote(amp.at[whole], ax.at[s, local], gsend.at[s, 2 + half], grecv_a.at[s, half], device)

        sized(half * PART, PART, quarter_of(dx), act)

    def send_near(kind, half):
        send(kind, half, 1, 0)
        send(kind, half, -1, 1)

    def via(way):
        return at(dx=1 - 2 * way)

    def start_v(way):
        def act(local, whole):
            dst = relay_v.at[way, pl.ds(0, local.size)]
            remote(itg.at[whole], dst, hsend_v.at[way], hrecv_v.at[way], via(way))

        sized(way * PART, PART, quarter_of(2), act)

    def pass_v(way):
        def act(local, _):
            src = relay_v.at[way, pl.ds(0, local.size)]
            wait(src, hrecv_v.at[way])
            remote(src, vx.at[2, local], rsend_v.at[way], grecv_v.at[2, way], via(way))

        sized(way * PART, PART, quarter_of(1 - 2 * way), act)

    def start_a(side, way):
        def act(local, whole):
            src = amp.at[whole, pl.ds(0, HALF)] if side == 0 else aside.at[local]
            dst = relay_a.at[side, way, pl.ds(0, local.size)]
            remote(src, dst, hsend_a.at[side, way], hrecv_a.at[side, way], via(way))

        sized(way * PART, PART, quarter_of(2), act)

    def pass_a(side, way):
        def act(local, _):
            src = relay_a.at[side, way, pl.ds(0, local.size)]
            wait(src, hrecv_a.at[side, way])
            remote(src, afar.at[side, local], rsend_a.at[side, way], far_recv.at[side, way], via(way))

        sized(way * PART, PART, quarter_of(1 - 2 * way), act)

    def forward(s, half):
        rows = pl.ds(half * PART, PART)
        remote(vx.at[s, rows], vz.at[s + 1, rows], fsend.at[s + 1, half], frecv.at[s + 1, half], at(dzl=1))

    limit = jnp.where(x == 3, QUARTER - SHORT, QUARTER)

    def known(value, start):
        index = lax.broadcasted_iota(jnp.int32, value.shape, 0) + start
        return jnp.where(index < limit, value, 0.0)

    def split_v(src, j, start, size, lanes=pl.ds(0, ROWS)):
        def step(c, _):
            at_row = pl.multiple_of(c * CHUNK, CHUNK)
            value = known(src[pl.ds(at_row, CHUNK)], start + at_row)
            high = value.astype(BF16)
            rows = pl.ds(pl.multiple_of(start + at_row, CHUNK), CHUNK)
            vhi[j, rows, lanes] = high
            vlo[j, rows, lanes] = (value - high.astype(F32)).astype(BF16)
            return 0

        lax.fori_loop(0, size // CHUNK, step, 0)

    def split_a(src, i, row0, start, size):
        rows = pl.ds(row0, src.shape[1])

        def step(c, _):
            at_row = pl.multiple_of(c * CHUNK, CHUNK)
            value = known(src[pl.ds(at_row, CHUNK)], start + at_row).T
            high = value.astype(BF16)
            columns = pl.ds(pl.multiple_of(start + at_row, CHUNK), CHUNK)
            ahi[i, rows, columns] = high
            alo[i, rows, columns] = (value - high.astype(F32)).astype(BF16)
            return 0

        lax.fori_loop(0, size // CHUNK, step, 0)

    def take_v(s, half):
        sized(half * PART, PART, x, lambda local, _: wait(vx.at[s, local], grecv_v.at[s, half]))
        if s < 2:
            forward(s, half)

    def forward_last(side):
        lanes = pl.ds(side * LANES, LANES)
        remote(vx.at[2, :, lanes], vz.at[3, :, lanes], fsend.at[3, side], frecv.at[3, side], at(dzl=1))

    def take_last(side):
        lanes = pl.ds(side * LANES, LANES)
        wait(vz.at[3, :, lanes], frecv.at[3, side])
        split_v(vz.at[3, :, lanes], 7, 0, QUARTER, lanes)

    def split_taken(s, half):
        split_v(vx.at[s, pl.ds(half * PART, PART)], s + 1, half * PART, PART)

    def take_z(s, half):
        rows = pl.ds(half * PART, PART)
        if s == 0:
            sized(half * PART, PART, x, lambda local, _: wait(vz.at[s, local], frecv.at[s, half]))
        else:
            wait(vz.at[s, rows], frecv.at[s, half])
        split_v(vz.at[s, rows], 4 + s, half * PART, PART)

    def take_a(s, half):
        sized(half * PART, PART, x, lambda local, _: wait(ax.at[s, local], grecv_a.at[s, half]))
        split_a(ax.at[s, pl.ds(half * PART, PART)], s + 1, 0, half * PART, PART)

    def take_far(side):
        for way in range(2):
            sized(way * PART, PART, x, lambda local, _: wait(afar.at[side, local], far_recv.at[side, way]))
        split_a(afar.at[side], 3, side * HALF, 0, QUARTER)

    def load_v(u, act):
        sized(u * UNIT, UNIT, x, lambda local, whole: act(
            itg.at[whole], stage_v.at[u % 2, pl.ds(0, local.size)], own_v.at[u % 2]))

    def load_a(u, act):
        sized(u % 4 * UNIT, UNIT, x if u < 4 else quarter_of(2), lambda local, whole: act(
            amp.at[whole], stage_a.at[u % 2, pl.ds(0, local.size)], own_a.at[u % 2]))

    def begin(src, dst, sem):
        pltpu.make_async_copy(src, dst, sem).start()

    def end(src, dst, sem):
        wait(dst, sem)

    def set_aside(u):
        def step(c, _):
            at_row = pl.multiple_of(c * CHUNK, CHUNK)
            n = amp.shape[1] - HALF
            aside[pl.ds(pl.multiple_of(u % 4 * UNIT + at_row, CHUNK), CHUNK), pl.ds(0, n)] = stage_a[
                u % 2, pl.ds(at_row, CHUNK), pl.ds(HALF, n)
            ]
            return 0

        lax.fori_loop(0, UNIT // CHUNK, step, 0)

    def rows_of(half):
        return pl.ds(0, ROWS) if half is None else pl.ds(half * HALF, HALF)

    def sem_row(i, half):
        return i if half is None else 3 + half

    def product(i, rows, n, high_v, low_v):
        high, low = ahi[i, rows], alo[i, rows]
        both = jnp.concatenate([high, low], axis=0)
        one = dot(both, high_v)
        if n == ROWS:
            return one[:n] + one[n:] + dot(high, low_v)
        two = dot(both, low_v)
        return one[:n] + one[n:] + two[:n] + two[n:]

    def produce(i, j, half, slot):
        rows = rows_of(half)
        n = ROWS if half is None else HALF
        value = product(i, rows, n, vhi[j], vlo[j])
        ptile[slot, 0, pl.ds(0, n)] = value[:, :LANES]
        ptile[slot, 1, pl.ds(0, n)] = value[:, LANES:]
        remote(
            ptile.at[slot, 1 - core, pl.ds(0, n)], crecv.at[j, i, rows],
            csend.at[slot], crecv_sem.at[j, sem_row(i, half)], at(dc=1),
        )

    def finish(i, j, half, own):
        rows = rows_of(half)
        n = ROWS if half is None else HALF
        wait(crecv.at[j, i, rows], crecv_sem.at[j, sem_row(i, half)])
        crecv[j, i, rows] += own[pl.ds(0, n)]
        d, zj = lax.rem(j, 4), j // 4
        shift = jnp.where(d == 0, 4, jnp.where(d == 1, 3, jnp.where(d == 2, 5, 6)))
        target = lax.rem(x + shift, 4)
        distance = lax.rem(y - target + 4, 4)

        @pl.when(distance != 0)
        def _():
            remote(
                crecv.at[j, i, rows], yrecv.at[distance - 1, zj, i, rows],
                ysend, yrecv_sem.at[distance - 1, zj, sem_row(i, half)],
                (occ, zh * 8 + target * 2 + core),
            )

    def tiles(count, n, index, half=None, free=0):
        def step(k, _):
            @pl.when(k < n)
            def _():
                i, j = index(k)
                slot = lax.rem(count + k, SLOTS)

                @pl.when(k >= free)
                def _():
                    wait(ptile.at[slot, 0, pl.ds(0, ROWS if half is None else HALF)], csend.at[slot])

                produce(i, j, half, slot)

            @pl.when(k > 0)
            def _():
                i, j = index(k - 1)
                finish(i, j, half, ptile.at[lax.rem(count + k - 1, SLOTS), core])

            return 0

        lax.fori_loop(0, n + 1, step, 0)

    def settle(n):
        for slot in range(SLOTS):
            wait(ptile.at[slot, 0, pl.ds(0, n)], csend.at[slot])

    def last_tiles(side, n, half=None):
        lanes = pl.ds(side * LANES, LANES)
        rows = rows_of(half)
        block = (lambda k: k) if half is None else (lambda k: 3)

        def step(k, _):
            @pl.when(k < n)
            def _():
                i = block(k)
                plast[side, i, rows] = product(i, rows, ROWS if half is None else HALF, vhi[7, :, lanes], vlo[7, :, lanes])

                @pl.when(core != side)
                def _():
                    remote(
                        plast.at[side, i, rows], crecv.at[7, i, rows],
                        lsend.at[side, sem_row(i, half)], crecv_sem.at[7, sem_row(i, half)], at(dc=1),
                    )

            @pl.when((k > 0) & (core == side))
            def _():
                i = block(k - 1)
                finish(i, 7, half, plast.at[side, i, rows])

            return 0

        lax.fori_loop(0, n + 1, step, 0)

    for half in range(2):
        send_near("v", half)
        sized(half * PART, PART, x, lambda local, whole, half=half: remote(
            itg.at[whole], vz.at[0, local], fsend.at[0, half], frecv.at[0, half], at(dzl=1)))
    for way in range(2):
        start_v(way)
    send_near("a", 0)
    send_near("a", 1)
    for u in range(2):
        load_v(u, begin)
        load_a(u, begin)
    for u in range(4):
        load_v(u, end)
        split_v(stage_v.at[u % 2], 0, u * UNIT, UNIT)
        if u < 2:
            load_v(u + 2, begin)
    for u in range(8):
        load_a(u, end)
        if u < 4:
            split_a(stage_a.at[u % 2], 0, 0, u * UNIT, UNIT)
        else:
            set_aside(u)
        if u < 6:
            load_a(u + 2, begin)

    take_v(0, 0)
    take_v(1, 0)
    split_taken(0, 0)
    split_taken(1, 0)
    take_z(0, 0)

    take_v(0, 1)
    take_v(1, 1)
    split_taken(0, 1)
    split_taken(1, 1)
    take_z(0, 1)
    tiles(0, 4, lambda k: (0, k + k // 3), free=4)

    take_a(0, 0)
    take_a(1, 0)
    take_z(1, 0)

    for way in range(2):
        pass_v(way)
    for side in range(2):
        for way in range(2):
            start_a(side, way)
    take_z(2, 0)

    take_a(0, 1)
    take_a(1, 1)
    tiles(4, 8, lambda k: (1 + k // 4, k % 4 + k % 4 // 3))
    take_z(1, 1)
    tiles(12, 3, lambda k: (k, 5))

    take_v(2, 0)
    take_v(2, 1)
    forward_last(0)
    forward_last(1)
    split_taken(2, 0)
    split_taken(2, 1)
    tiles(15, 3, lambda k: (k, 3))
    take_z(2, 1)
    tiles(18, 3, lambda k: (k, 6))

    mine = lax.rem(y - x + 4, 4)
    mine = jnp.where(mine == 0, 0, jnp.where(mine == 3, 1, jnp.where(mine == 1, 2, 3)))

    def collect(zj, i, half=None):
        row = sem_row(i, half)
        start = 0 if half is None else half * HALF
        for s in range(3):
            wait(yrecv.at[s, zj, i, rows_of(half)], yrecv_sem.at[s, zj, row])

        def step(c, _):
            rows = pl.ds(pl.multiple_of(start + c * 32, 32), 32)
            total[zj, i, rows] = (crecv[zj * 4 + mine, i, rows] + yrecv[0, zj, i, rows]) + (
                yrecv[1, zj, i, rows] + yrecv[2, zj, i, rows]
            )
            return 0

        lax.fori_loop(0, (ROWS if half is None else HALF) // 32, step, 0)
        if i > 0:
            s, rows = (None, 1, 0, 2)[i], rows_of(half)
            remote(
                total.at[zj, i, rows], xrecv.at[s, zj, rows],
                osend.at[row - 1, zj], orecv.at[row - 1, zj], at(dx=OFFSET[i]),
            )

    late = mine == 3

    for way in range(2):
        pass_a(0, way)
    for i in (1, 2, 0):
        collect(0, i)

    @pl.when(~late)
    def _():
        for i in (1, 2, 0):
            collect(1, i)

    for way in range(2):
        pass_a(1, way)
    take_last(0)
    last_tiles(0, 3)
    take_far(0)
    settle(ROWS)
    tiles(0, 7, lambda k: (3, k), half=0, free=SLOTS)
    last_tiles(0, 1, half=0)
    collect(0, 3, 0)

    @pl.when(~late)
    def _():
        collect(1, 3, 0)

    @pl.when(late & (core == 0))
    def _():
        for i in (1, 2, 0):
            collect(1, i)
        collect(1, 3, 0)

    settle(HALF)
    take_last(1)
    last_tiles(1, 3)
    last_tiles(1, 1, half=0)
    take_far(1)
    tiles(0, 8, lambda k: (3, k), half=1, free=SLOTS)

    @pl.when(late & (core == 1))
    def _():
        for i in (1, 2, 0):
            collect(1, i)
        collect(1, 3, 0)

    collect(0, 3, 1)
    collect(1, 3, 1)

    keep = lax.rem(zl + zh, 2)
    parts = [(i, None) for i in (1, 2)] + [(3, half) for half in range(2)]
    for zj in range(2):
        for i, half in parts:
            wait(xrecv.at[(None, 1, 0, 2)[i], zj, rows_of(half)], orecv.at[sem_row(i, half) - 1, zj])

    def summed(zj):
        return (total[zj, 0] + xrecv[0, zj]) + (xrecv[1, zj] + xrecv[2, zj])

    zsend[...] = summed(1 - keep)
    remote(zsend, zrecv, zsem.at[0], zsem.at[1], at(dzh=1))
    result = summed(keep)[: out.shape[0]]
    wait(zrecv, zsem.at[1])
    out[...] = result + zrecv[: out.shape[0]]

    wait(zsend, zsem.at[0])
    wait(yrecv, ysend)
    settle(HALF)
    for zj in range(2):
        for i, half in parts:
            wait(total.at[zj, i, rows_of(half)], osend.at[sem_row(i, half) - 1, zj])
    for side in range(2):

        @pl.when(core != side)
        def _():
            for i, half in [(0, None)] + parts[:3]:
                wait(plast.at[side, i, rows_of(half)], lsend.at[side, sem_row(i, half)])

    for half in range(2):
        for s, dx in enumerate((1, -1)):
            sized(half * PART, PART, quarter_of(dx), lambda local, _: wait(vx.at[s, local], gsend.at[s, half]))
            sized(half * PART, PART, quarter_of(dx), lambda local, _: wait(ax.at[s, local], gsend.at[s, 2 + half]))
        way = half
        sized(way * PART, PART, quarter_of(2), lambda local, _: wait(vx.at[2, local], hsend_v.at[way]))
        sized(way * PART, PART, quarter_of(1 - 2 * way), lambda local, _: wait(vx.at[2, local], rsend_v.at[way]))
        for side in range(2):
            sized(way * PART, PART, quarter_of(2), lambda local, _: wait(afar.at[side, local], hsend_a.at[side, way]))
            sized(way * PART, PART, quarter_of(1 - 2 * way), lambda local, _: wait(afar.at[side, local], rsend_a.at[side, way]))
    for half in range(2):
        sized(half * PART, PART, x, lambda local, _: wait(vz.at[0, local], fsend.at[0, half]))
        for s in range(1, 4):
            wait(vz.at[s, pl.ds(half * PART, PART)], fsend.at[s, half])


def body(integrals, amplitudes, residual_in):
    rows = amplitudes.shape[0]
    any_spec = pl.BlockSpec(memory_space=pl.ANY)
    vmem_spec = pl.BlockSpec(memory_space=pltpu.VMEM)
    dma = pltpu.SemaphoreType.DMA
    ladder = pl.pallas_call(
        kernel,
        name="ladder",
        out_shape=(
            jax.ShapeDtypeStruct(residual_in.shape, F32),
            jax.ShapeDtypeStruct((2, PART, ROWS), F32),
            jax.ShapeDtypeStruct((2, 2, PART, HALF), F32),
        ),
        in_specs=[any_spec] * 2,
        out_specs=(vmem_spec, any_spec, any_spec),
        scratch_shapes=[
            pltpu.VMEM((3, QUARTER, ROWS), F32),
            pltpu.VMEM((4, QUARTER, ROWS), F32),
            pltpu.VMEM((2, QUARTER, rows), F32),
            pltpu.VMEM((2, QUARTER, HALF), F32),
            pltpu.VMEM((QUARTER, HALF), F32),
            pltpu.VMEM((2, UNIT, ROWS), F32),
            pltpu.VMEM((2, UNIT, rows), F32),
            pltpu.VMEM((8, QUARTER, ROWS), BF16),
            pltpu.VMEM((8, QUARTER, ROWS), BF16),
            pltpu.VMEM((4, ROWS, QUARTER), BF16),
            pltpu.VMEM((4, ROWS, QUARTER), BF16),
            pltpu.VMEM((SLOTS, 2, ROWS, LANES), F32),
            pltpu.VMEM((2, 4, ROWS, LANES), F32),
            pltpu.VMEM((8, 4, ROWS, LANES), F32),
            pltpu.VMEM((3, 2, 4, ROWS, LANES), F32),
            pltpu.VMEM((3, 2, ROWS, LANES), F32),
            pltpu.VMEM((2, 4, ROWS, LANES), F32),
            pltpu.VMEM((ROWS, LANES), F32),
            pltpu.VMEM((ROWS, LANES), F32),
            dma((2,)),
            dma((2,)),
            dma((2, 4)),
            dma((3, 2)),
            dma((2, 2)),
            dma((2,)),
            dma((2,)),
            dma((2, 2)),
            dma((2, 2)),
            dma((2,)),
            dma((2, 2)),
            dma((2, 2)),
            dma((4, 2)),
            dma((4, 2)),
            dma((SLOTS,)),
            dma((2, 5)),
            dma((8, 5)),
            dma,
            dma((3, 2, 5)),
            dma((4, 2)),
            dma((4, 2)),
            dma((2,)),
        ],
        compiler_params=pltpu.CompilerParams(
            collective_id=0, has_side_effects=True, vmem_limit_bytes=61 * 2**20
        ),
        cost_estimate=pl.CostEstimate(flops=3 * 2 * 1008 * 2048 * 2048, bytes_accessed=2 * 2**24, transcendentals=0),
    )(amplitudes.T, integrals.T)[0]
    return residual_in + ladder


def solution(mesh):
    return jax.shard_map(
        body,
        mesh=mesh,
        in_specs=(P("occ", "vir"), P("occ", "vir"), P("occ", "vir")),
        out_specs=P("occ", "vir"),
        check_vma=False,
    )
```

```python
import jax
import jax.numpy as jnp
from jax import lax
from jax.experimental import pallas as pl
from jax.experimental.pallas import tpu as pltpu
from jax.sharding import PartitionSpec as P

MESH = pl.DeviceIdType.MESH
F32, BF16 = jnp.float32, jnp.bfloat16

ROWS, HALF, LANES = 256, 128, 128
QUARTER, PART, UNIT, CHUNK = 2048, 1024, 512, 128
SHORT = 16
SLOTS = 4

OFFSET = (0, -1, 1, 2)


def dot(a, b):
    return jnp.dot(a, b, preferred_element_type=F32)


def kernel(
    amp, itg, out, relay_v, relay_a,
    vx, vz, ax, afar, aside, stage_v, stage_a, vhi, vlo, ahi, alo, ptile, plast, crecv, yrecv, xrecv, total, zsend, zrecv,
    own_v, own_a, gsend, grecv_v, grecv_a, hsend_v, hrecv_v, hsend_a, hrecv_a, rsend_v, rsend_a, far_recv, fsend, frecv, csend, lsend, crecv_sem, ysend, yrecv_sem,
    osend, orecv, zsem,
):
    occ, vir = lax.axis_index("occ"), lax.axis_index("vir")
    x, zl = lax.rem(occ, 4), occ // 4
    core, y, zh = lax.rem(vir, 2), lax.rem(vir // 2, 4), vir // 8

    def at(dx=0, dzl=0, dy=0, dzh=0, dc=0):
        return (
            lax.rem(zl + dzl, 2) * 4 + lax.rem(x + dx + 4, 4),
            lax.rem(zh + dzh, 2) * 8 + lax.rem(y + dy + 4, 4) * 2 + lax.rem(core + dc, 2),
        )

    peers = [at(dx=1), at(dx=-1), at(dx=2), at(dzl=1), at(dc=1), at(dy=1), at(dy=-1), at(dy=2), at(dzh=1)]
    barrier = pltpu.get_barrier_semaphore()
    for peer in peers:
        pl.semaphore_signal(barrier, inc=1, device_id=peer, device_id_type=MESH)
    pl.semaphore_wait(barrier, len(peers))

    def remote(src, dst, ssem, rsem, device):
        pltpu.make_async_remote_copy(
            src_ref=src, dst_ref=dst, send_sem=ssem, recv_sem=rsem, device_id=device, device_id_type=MESH
        ).start()

    def wait(ref, sem):
        pltpu.make_async_copy(ref, ref, sem).wait()

    def sized(start, size, quarter, act):
        if start + size < QUARTER:
            act(pl.ds(start, size), pl.ds(pl.multiple_of(quarter * QUARTER + start, SHORT), size))
        else:

            @pl.when(quarter != 3)
            def _():
                act(pl.ds(start, size), pl.ds(pl.multiple_of(quarter * QUARTER + start, SHORT), size))

            @pl.when(quarter == 3)
            def _():
                act(pl.ds(start, size - SHORT), pl.ds(3 * QUARTER + start, size - SHORT))

    def quarter_of(dx):
        return lax.rem(x + dx + 4, 4)

    def send(kind, half, dx, s):
        device = at(dx=dx)

        def act(local, whole):
            if kind == "v":
                remote(itg.at[whole], vx.at[s, local], gsend.at[s, half], grecv_v.at[s, half], device)
            else:
                remote(amp.at[whole], ax.at[s, local], gsend.at[s, 2 + half], grecv_a.at[s, half], device)

        sized(half * PART, PART, quarter_of(dx), act)

    def send_near(kind, half):
        send(kind, half, 1, 0)
        send(kind, half, -1, 1)

    def via(way):
        return at(dx=1 - 2 * way)

    def start_v(way):
        def act(local, whole):
            dst = relay_v.at[way, pl.ds(0, local.size)]
            remote(itg.at[whole], dst, hsend_v.at[way], hrecv_v.at[way], via(way))

        sized(way * PART, PART, quarter_of(2), act)

    def pass_v(way):
        def act(local, _):
            src = relay_v.at[way, pl.ds(0, local.size)]
            wait(src, hrecv_v.at[way])
            remote(src, vx.at[2, local], rsend_v.at[way], grecv_v.at[2, way], via(way))

        sized(way * PART, PART, quarter_of(1 - 2 * way), act)

    def start_a(side, way):
        def act(local, whole):
            src = amp.at[whole, pl.ds(0, HALF)] if side == 0 else aside.at[local]
            dst = relay_a.at[side, way, pl.ds(0, local.size)]
            remote(src, dst, hsend_a.at[side, way], hrecv_a.at[side, way], via(way))

        sized(way * PART, PART, quarter_of(2), act)

    def pass_a(side, way):
        def act(local, _):
            src = relay_a.at[side, way, pl.ds(0, local.size)]
            wait(src, hrecv_a.at[side, way])
            remote(src, afar.at[side, local], rsend_a.at[side, way], far_recv.at[side, way], via(way))

        sized(way * PART, PART, quarter_of(1 - 2 * way), act)

    def forward(s, half):
        rows = pl.ds(half * PART, PART)
        remote(vx.at[s, rows], vz.at[s + 1, rows], fsend.at[s + 1, half], frecv.at[s + 1, half], at(dzl=1))

    limit = jnp.where(x == 3, QUARTER - SHORT, QUARTER)

    def known(value, start):
        index = lax.broadcasted_iota(jnp.int32, value.shape, 0) + start
        return jnp.where(index < limit, value, 0.0)

    def split_v(src, j, start, size, lanes=pl.ds(0, ROWS)):
        def step(c, _):
            at_row = pl.multiple_of(c * CHUNK, CHUNK)
            value = known(src[pl.ds(at_row, CHUNK)], start + at_row)
            high = value.astype(BF16)
            rows = pl.ds(pl.multiple_of(start + at_row, CHUNK), CHUNK)
            vhi[j, rows, lanes] = high
            vlo[j, rows, lanes] = (value - high.astype(F32)).astype(BF16)
            return 0

        lax.fori_loop(0, size // CHUNK, step, 0)

    def split_a(src, i, row0, start, size):
        rows = pl.ds(row0, src.shape[1])

        def step(c, _):
            at_row = pl.multiple_of(c * CHUNK, CHUNK)
            value = known(src[pl.ds(at_row, CHUNK)], start + at_row).T
            high = value.astype(BF16)
            columns = pl.ds(pl.multiple_of(start + at_row, CHUNK), CHUNK)
            ahi[i, rows, columns] = high
            alo[i, rows, columns] = (value - high.astype(F32)).astype(BF16)
            return 0

        lax.fori_loop(0, size // CHUNK, step, 0)

    def take_v(s, half):
        sized(half * PART, PART, x, lambda local, _: wait(vx.at[s, local], grecv_v.at[s, half]))
        if s < 2:
            forward(s, half)

    def forward_last(side):
        lanes = pl.ds(side * LANES, LANES)
        remote(vx.at[2, :, lanes], vz.at[3, :, lanes], fsend.at[3, side], frecv.at[3, side], at(dzl=1))

    def take_last(side):
        lanes = pl.ds(side * LANES, LANES)
        wait(vz.at[3, :, lanes], frecv.at[3, side])
        split_v(vz.at[3, :, lanes], 7, 0, QUARTER, lanes)

    def split_taken(s, half):
        split_v(vx.at[s, pl.ds(half * PART, PART)], s + 1, half * PART, PART)

    def take_z(s, half):
        rows = pl.ds(half * PART, PART)
        if s == 0:
            sized(half * PART, PART, x, lambda local, _: wait(vz.at[s, local], frecv.at[s, half]))
        else:
            wait(vz.at[s, rows], frecv.at[s, half])
        split_v(vz.at[s, rows], 4 + s, half * PART, PART)

    def take_a(s, half):
        sized(half * PART, PART, x, lambda local, _: wait(ax.at[s, local], grecv_a.at[s, half]))
        split_a(ax.at[s, pl.ds(half * PART, PART)], s + 1, 0, half * PART, PART)

    def take_far(side):
        for way in range(2):
            sized(way * PART, PART, x, lambda local, _: wait(afar.at[side, local], far_recv.at[side, way]))
        split_a(afar.at[side], 3, side * HALF, 0, QUARTER)

    def load_v(u, act):
        sized(u * UNIT, UNIT, x, lambda local, whole: act(
            itg.at[whole], stage_v.at[u % 2, pl.ds(0, local.size)], own_v.at[u % 2]))

    def load_a(u, act):
        sized(u % 4 * UNIT, UNIT, x if u < 4 else quarter_of(2), lambda local, whole: act(
            amp.at[whole], stage_a.at[u % 2, pl.ds(0, local.size)], own_a.at[u % 2]))

    def begin(src, dst, sem):
        pltpu.make_async_copy(src, dst, sem).start()

    def end(src, dst, sem):
        wait(dst, sem)

    def set_aside(u):
        def step(c, _):
            at_row = pl.multiple_of(c * CHUNK, CHUNK)
            n = amp.shape[1] - HALF
            aside[pl.ds(pl.multiple_of(u % 4 * UNIT + at_row, CHUNK), CHUNK), pl.ds(0, n)] = stage_a[
                u % 2, pl.ds(at_row, CHUNK), pl.ds(HALF, n)
            ]
            return 0

        lax.fori_loop(0, UNIT // CHUNK, step, 0)

    def rows_of(half):
        return pl.ds(0, ROWS) if half is None else pl.ds(half * HALF, HALF)

    def sem_row(i, half):
        return i if half is None else 3 + half

    def product(i, rows, n, high_v, low_v):
        high, low = ahi[i, rows], alo[i, rows]
        both = jnp.concatenate([high, low], axis=0)
        one = dot(both, high_v)
        if n == ROWS:
            return one[:n] + one[n:] + dot(high, low_v)
        two = dot(both, low_v)
        return one[:n] + one[n:] + two[:n] + two[n:]

    def produce(i, j, half, slot):
        rows = rows_of(half)
        n = ROWS if half is None else HALF
        value = product(i, rows, n, vhi[j], vlo[j])
        ptile[slot, 0, pl.ds(0, n)] = value[:, :LANES]
        ptile[slot, 1, pl.ds(0, n)] = value[:, LANES:]
        remote(
            ptile.at[slot, 1 - core, pl.ds(0, n)], crecv.at[j, i, rows],
            csend.at[slot], crecv_sem.at[j, sem_row(i, half)], at(dc=1),
        )

    def finish(i, j, half, own):
        rows = rows_of(half)
        n = ROWS if half is None else HALF
        wait(crecv.at[j, i, rows], crecv_sem.at[j, sem_row(i, half)])
        crecv[j, i, rows] += own[pl.ds(0, n)]
        d, zj = lax.rem(j, 4), j // 4
        shift = jnp.where(d == 0, 4, jnp.where(d == 1, 3, jnp.where(d == 2, 5, 6)))
        target = lax.rem(x + shift, 4)
        distance = lax.rem(y - target + 4, 4)

        @pl.when(distance != 0)
        def _():
            remote(
                crecv.at[j, i, rows], yrecv.at[distance - 1, zj, i, rows],
                ysend, yrecv_sem.at[distance - 1, zj, sem_row(i, half)],
                (occ, zh * 8 + target * 2 + core),
            )

    def tiles(count, n, index, half=None, free=0):
        def step(k, _):
            @pl.when(k < n)
            def _():
                i, j = index(k)
                slot = lax.rem(count + k, SLOTS)

                @pl.when(k >= free)
                def _():
                    wait(ptile.at[slot, 0, pl.ds(0, ROWS if half is None else HALF)], csend.at[slot])

                produce(i, j, half, slot)

            @pl.when(k > 0)
            def _():
                i, j = index(k - 1)
                finish(i, j, half, ptile.at[lax.rem(count + k - 1, SLOTS), core])

            return 0

        lax.fori_loop(0, n + 1, step, 0)

    def settle(n):
        for slot in range(SLOTS):
            wait(ptile.at[slot, 0, pl.ds(0, n)], csend.at[slot])

    def last_tiles(side, n, half=None):
        lanes = pl.ds(side * LANES, LANES)
        rows = rows_of(half)
        block = (lambda k: k) if half is None else (lambda k: 3)

        def step(k, _):
            @pl.when(k < n)
            def _():
                i = block(k)
                plast[side, i, rows] = product(i, rows, ROWS if half is None else HALF, vhi[7, :, lanes], vlo[7, :, lanes])

                @pl.when(core != side)
                def _():
                    remote(
                        plast.at[side, i, rows], crecv.at[7, i, rows],
                        lsend.at[side, sem_row(i, half)], crecv_sem.at[7, sem_row(i, half)], at(dc=1),
                    )

            @pl.when((k > 0) & (core == side))
            def _():
                i = block(k - 1)
                finish(i, 7, half, plast.at[side, i, rows])

            return 0

        lax.fori_loop(0, n + 1, step, 0)

    for half in range(2):
        send_near("v", half)
        sized(half * PART, PART, x, lambda local, whole, half=half: remote(
            itg.at[whole], vz.at[0, local], fsend.at[0, half], frecv.at[0, half], at(dzl=1)))
    for way in range(2):
        start_v(way)
    send_near("a", 0)
    send_near("a", 1)
    for u in range(2):
        load_v(u, begin)
        load_a(u, begin)
    for u in range(4):
        load_v(u, end)
        split_v(stage_v.at[u % 2], 0, u * UNIT, UNIT)
        if u < 2:
            load_v(u + 2, begin)
    for u in range(8):
        load_a(u, end)
        if u < 4:
            split_a(stage_a.at[u % 2], 0, 0, u * UNIT, UNIT)
        else:
            set_aside(u)
        if u < 6:
            load_a(u + 2, begin)

    take_v(0, 0)
    take_v(1, 0)
    split_taken(0, 0)
    split_taken(1, 0)
    take_z(0, 0)

    take_v(0, 1)
    take_v(1, 1)
    split_taken(0, 1)
    split_taken(1, 1)
    take_z(0, 1)
    tiles(0, 4, lambda k: (0, k + k // 3), free=4)

    take_a(0, 0)
    take_a(1, 0)
    take_z(1, 0)

    for way in range(2):
        pass_v(way)
    for side in range(2):
        for way in range(2):
            start_a(side, way)
    take_z(2, 0)

    take_a(0, 1)
    take_a(1, 1)
    tiles(4, 8, lambda k: (1 + k // 4, k % 4 + k % 4 // 3))
    take_z(1, 1)
    tiles(12, 3, lambda k: (k, 5))

    take_v(2, 0)
    take_v(2, 1)
    forward_last(0)
    forward_last(1)
    split_taken(2, 0)
    split_taken(2, 1)
    tiles(15, 3, lambda k: (k, 3))
    take_z(2, 1)
    tiles(18, 3, lambda k: (k, 6))

    mine = lax.rem(y - x + 4, 4)
    mine = jnp.where(mine == 0, 0, jnp.where(mine == 3, 1, jnp.where(mine == 1, 2, 3)))

    def collect(zj, i, half=None):
        row = sem_row(i, half)
        start = 0 if half is None else half * HALF
        for s in range(3):
            wait(yrecv.at[s, zj, i, rows_of(half)], yrecv_sem.at[s, zj, row])

        def step(c, _):
            rows = pl.ds(pl.multiple_of(start + c * 32, 32), 32)
            total[zj, i, rows] = (crecv[zj * 4 + mine, i, rows] + yrecv[0, zj, i, rows]) + (
                yrecv[1, zj, i, rows] + yrecv[2, zj, i, rows]
            )
            return 0

        lax.fori_loop(0, (ROWS if half is None else HALF) // 32, step, 0)
        if i > 0:
            s, rows = (None, 1, 0, 2)[i], rows_of(half)
            remote(
                total.at[zj, i, rows], xrecv.at[s, zj, rows],
                osend.at[row - 1, zj], orecv.at[row - 1, zj], at(dx=OFFSET[i]),
            )

    late = mine == 3

    for way in range(2):
        pass_a(0, way)
    for i in (1, 2, 0):
        collect(0, i)

    @pl.when(~late)
    def _():
        for i in (1, 2, 0):
            collect(1, i)

    for way in range(2):
        pass_a(1, way)
    take_last(0)
    last_tiles(0, 3)
    take_far(0)
    settle(ROWS)
    tiles(0, 7, lambda k: (3, k), half=0, free=SLOTS)
    last_tiles(0, 1, half=0)
    collect(0, 3, 0)

    @pl.when(~late)
    def _():
        collect(1, 3, 0)

    @pl.when(late & (core == 0))
    def _():
        for i in (1, 2, 0):
            collect(1, i)
        collect(1, 3, 0)

    settle(HALF)
    take_last(1)
    last_tiles(1, 3)
    last_tiles(1, 1, half=0)
    take_far(1)
    tiles(0, 8, lambda k: (3, k), half=1, free=SLOTS)

    @pl.when(late & (core == 1))
    def _():
        for i in (1, 2, 0):
            collect(1, i)
        collect(1, 3, 0)

    collect(0, 3, 1)
    collect(1, 3, 1)

    keep = lax.rem(zl + zh, 2)
    parts = [(i, None) for i in (1, 2)] + [(3, half) for half in range(2)]
    def arrived(zj, some):
        for i, half in some:
            wait(xrecv.at[(None, 1, 0, 2)[i], zj, rows_of(half)], orecv.at[sem_row(i, half) - 1, zj])

    def summed(zj, rows):
        return (total[zj, 0, rows] + xrecv[0, zj, rows]) + (xrecv[1, zj, rows] + xrecv[2, zj, rows])

    for half in range(2):
        rows = rows_of(half)
        arrived(1 - keep, parts[:3] if half == 0 else parts[3:])
        zsend[rows] = summed(1 - keep, rows)
        remote(zsend.at[rows], zrecv.at[rows], zsem.at[0, half], zsem.at[1, half], at(dzh=1))
    arrived(keep, parts)
    result = summed(keep, rows_of(None))[: out.shape[0]]
    for half in range(2):
        wait(zrecv.at[rows_of(half)], zsem.at[1, half])
    out[...] = result + zrecv[: out.shape[0]]

    for half in range(2):
        wait(zsend.at[rows_of(half)], zsem.at[0, half])
    wait(yrecv, ysend)
    settle(HALF)
    for zj in range(2):
        for i, half in parts:
            wait(total.at[zj, i, rows_of(half)], osend.at[sem_row(i, half) - 1, zj])
    for side in range(2):

        @pl.when(core != side)
        def _():
            for i, half in [(0, None)] + parts[:3]:
                wait(plast.at[side, i, rows_of(half)], lsend.at[side, sem_row(i, half)])

    for half in range(2):
        for s, dx in enumerate((1, -1)):
            sized(half * PART, PART, quarter_of(dx), lambda local, _: wait(vx.at[s, local], gsend.at[s, half]))
            sized(half * PART, PART, quarter_of(dx), lambda local, _: wait(ax.at[s, local], gsend.at[s, 2 + half]))
        way = half
        sized(way * PART, PART, quarter_of(2), lambda local, _: wait(vx.at[2, local], hsend_v.at[way]))
        sized(way * PART, PART, quarter_of(1 - 2 * way), lambda local, _: wait(vx.at[2, local], rsend_v.at[way]))
        for side in range(2):
            sized(way * PART, PART, quarter_of(2), lambda local, _: wait(afar.at[side, local], hsend_a.at[side, way]))
            sized(way * PART, PART, quarter_of(1 - 2 * way), lambda local, _: wait(afar.at[side, local], rsend_a.at[side, way]))
    for half in range(2):
        sized(half * PART, PART, x, lambda local, _: wait(vz.at[0, local], fsend.at[0, half]))
        for s in range(1, 4):
            wait(vz.at[s, pl.ds(half * PART, PART)], fsend.at[s, half])


def body(integrals, amplitudes, residual_in):
    rows = amplitudes.shape[0]
    any_spec = pl.BlockSpec(memory_space=pl.ANY)
    vmem_spec = pl.BlockSpec(memory_space=pltpu.VMEM)
    dma = pltpu.SemaphoreType.DMA
    ladder = pl.pallas_call(
        kernel,
        name="ladder",
        out_shape=(
            jax.ShapeDtypeStruct(residual_in.shape, F32),
            jax.ShapeDtypeStruct((2, PART, ROWS), F32),
            jax.ShapeDtypeStruct((2, 2, PART, HALF), F32),
        ),
        in_specs=[any_spec] * 2,
        out_specs=(vmem_spec, any_spec, any_spec),
        scratch_shapes=[
            pltpu.VMEM((3, QUARTER, ROWS), F32),
            pltpu.VMEM((4, QUARTER, ROWS), F32),
            pltpu.VMEM((2, QUARTER, rows), F32),
            pltpu.VMEM((2, QUARTER, HALF), F32),
            pltpu.VMEM((QUARTER, HALF), F32),
            pltpu.VMEM((2, UNIT, ROWS), F32),
            pltpu.VMEM((2, UNIT, rows), F32),
            pltpu.VMEM((8, QUARTER, ROWS), BF16),
            pltpu.VMEM((8, QUARTER, ROWS), BF16),
            pltpu.VMEM((4, ROWS, QUARTER), BF16),
            pltpu.VMEM((4, ROWS, QUARTER), BF16),
            pltpu.VMEM((SLOTS, 2, ROWS, LANES), F32),
            pltpu.VMEM((2, 4, ROWS, LANES), F32),
            pltpu.VMEM((8, 4, ROWS, LANES), F32),
            pltpu.VMEM((3, 2, 4, ROWS, LANES), F32),
            pltpu.VMEM((3, 2, ROWS, LANES), F32),
            pltpu.VMEM((2, 4, ROWS, LANES), F32),
            pltpu.VMEM((ROWS, LANES), F32),
            pltpu.VMEM((ROWS, LANES), F32),
            dma((2,)),
            dma((2,)),
            dma((2, 4)),
            dma((3, 2)),
            dma((2, 2)),
            dma((2,)),
            dma((2,)),
            dma((2, 2)),
            dma((2, 2)),
            dma((2,)),
            dma((2, 2)),
            dma((2, 2)),
            dma((4, 2)),
            dma((4, 2)),
            dma((SLOTS,)),
            dma((2, 5)),
            dma((8, 5)),
            dma,
            dma((3, 2, 5)),
            dma((4, 2)),
            dma((4, 2)),
            dma((2, 2)),
        ],
        compiler_params=pltpu.CompilerParams(
            collective_id=0, has_side_effects=True, vmem_limit_bytes=61 * 2**20
        ),
        cost_estimate=pl.CostEstimate(flops=3 * 2 * 1008 * 2048 * 2048, bytes_accessed=2 * 2**24, transcendentals=0),
    )(amplitudes.T, integrals.T)[0]
    return residual_in + ladder


def solution(mesh):
    return jax.shard_map(
        body,
        mesh=mesh,
        in_specs=(P("occ", "vir"), P("occ", "vir"), P("occ", "vir")),
        out_specs=P("occ", "vir"),
        check_vma=False,
    )
```

```python
import jax
import jax.numpy as jnp
from jax import lax
from jax.experimental import pallas as pl
from jax.experimental.pallas import tpu as pltpu
from jax.sharding import PartitionSpec as P

MESH = pl.DeviceIdType.MESH
F32, BF16 = jnp.float32, jnp.bfloat16

ROWS, HALF, LANES = 256, 128, 128
QUARTER, PART, UNIT, CHUNK = 2048, 1024, 512, 128
SHORT = 16
SLOTS = 4

OFFSET = (0, -1, 1, 2)


def dot(a, b):
    return jnp.dot(a, b, preferred_element_type=F32)


def kernel(
    amp, itg, out, relay_v, relay_a,
    vx, vz, ax, afar, aside, stage_v, stage_a, vhi, vlo, ahi, alo, ptile, plast, crecv, yrecv, xrecv, total, zsend, zrecv,
    own_v, own_a, gsend, grecv_v, grecv_a, hsend_v, hrecv_v, hsend_a, hrecv_a, rsend_v, rsend_a, far_recv, fsend, frecv, csend, lsend, crecv_sem, ysend, yrecv_sem,
    osend, orecv, zsem,
):
    occ, vir = lax.axis_index("occ"), lax.axis_index("vir")
    x, zl = lax.rem(occ, 4), occ // 4
    core, y, zh = lax.rem(vir, 2), lax.rem(vir // 2, 4), vir // 8

    def at(dx=0, dzl=0, dy=0, dzh=0, dc=0):
        return (
            lax.rem(zl + dzl, 2) * 4 + lax.rem(x + dx + 4, 4),
            lax.rem(zh + dzh, 2) * 8 + lax.rem(y + dy + 4, 4) * 2 + lax.rem(core + dc, 2),
        )

    peers = [at(dx=1), at(dx=-1), at(dx=2), at(dzl=1), at(dc=1), at(dy=1), at(dy=-1), at(dy=2), at(dzh=1)]
    barrier = pltpu.get_barrier_semaphore()
    for peer in peers:
        pl.semaphore_signal(barrier, inc=1, device_id=peer, device_id_type=MESH)
    pl.semaphore_wait(barrier, len(peers))

    def remote(src, dst, ssem, rsem, device):
        pltpu.make_async_remote_copy(
            src_ref=src, dst_ref=dst, send_sem=ssem, recv_sem=rsem, device_id=device, device_id_type=MESH
        ).start()

    def wait(ref, sem):
        pltpu.make_async_copy(ref, ref, sem).wait()

    def sized(start, size, quarter, act):
        if start + size < QUARTER:
            act(pl.ds(start, size), pl.ds(pl.multiple_of(quarter * QUARTER + start, SHORT), size))
        else:

            @pl.when(quarter != 3)
            def _():
                act(pl.ds(start, size), pl.ds(pl.multiple_of(quarter * QUARTER + start, SHORT), size))

            @pl.when(quarter == 3)
            def _():
                act(pl.ds(start, size - SHORT), pl.ds(3 * QUARTER + start, size - SHORT))

    def quarter_of(dx):
        return lax.rem(x + dx + 4, 4)

    def send(kind, half, dx, s):
        device = at(dx=dx)

        def act(local, whole):
            if kind == "v":
                remote(itg.at[whole], vx.at[s, local], gsend.at[s, half], grecv_v.at[s, half], device)
            else:
                remote(amp.at[whole], ax.at[s, local], gsend.at[s, 2 + half], grecv_a.at[s, half], device)

        sized(half * PART, PART, quarter_of(dx), act)

    def send_near(kind, half):
        send(kind, half, 1, 0)
        send(kind, half, -1, 1)

    def via(way):
        return at(dx=1 - 2 * way)

    def start_v(way):
        def act(local, whole):
            dst = relay_v.at[way, pl.ds(0, local.size)]
            remote(itg.at[whole], dst, hsend_v.at[way], hrecv_v.at[way], via(way))

        sized(way * PART, PART, quarter_of(2), act)

    def pass_v(way):
        def act(local, _):
            src = relay_v.at[way, pl.ds(0, local.size)]
            wait(src, hrecv_v.at[way])
            remote(src, vx.at[2, local], rsend_v.at[way], grecv_v.at[2, way], via(way))

        sized(way * PART, PART, quarter_of(1 - 2 * way), act)

    def start_a(side, way):
        def act(local, whole):
            src = amp.at[whole, pl.ds(0, HALF)] if side == 0 else aside.at[local]
            dst = relay_a.at[side, way, pl.ds(0, local.size)]
            remote(src, dst, hsend_a.at[side, way], hrecv_a.at[side, way], via(way))

        sized(way * PART, PART, quarter_of(2), act)

    def pass_a(side, way):
        def act(local, _):
            src = relay_a.at[side, way, pl.ds(0, local.size)]
            wait(src, hrecv_a.at[side, way])
            remote(src, afar.at[side, local], rsend_a.at[side, way], far_recv.at[side, way], via(way))

        sized(way * PART, PART, quarter_of(1 - 2 * way), act)

    def forward(s, half):
        rows = pl.ds(half * PART, PART)
        remote(vx.at[s, rows], vz.at[s + 1, rows], fsend.at[s + 1, half], frecv.at[s + 1, half], at(dzl=1))

    limit = jnp.where(x == 3, QUARTER - SHORT, QUARTER)

    def known(value, start):
        index = lax.broadcasted_iota(jnp.int32, value.shape, 0) + start
        return jnp.where(index < limit, value, 0.0)

    def split_v(src, j, start, size, lanes=pl.ds(0, ROWS)):
        def step(c, _):
            at_row = pl.multiple_of(c * CHUNK, CHUNK)
            value = known(src[pl.ds(at_row, CHUNK)], start + at_row)
            high = value.astype(BF16)
            rows = pl.ds(pl.multiple_of(start + at_row, CHUNK), CHUNK)
            vhi[j, rows, lanes] = high
            vlo[j, rows, lanes] = (value - high.astype(F32)).astype(BF16)
            return 0

        lax.fori_loop(0, size // CHUNK, step, 0)

    def split_a(src, i, row0, start, size):
        rows = pl.ds(row0, src.shape[1])

        def step(c, _):
            at_row = pl.multiple_of(c * CHUNK, CHUNK)
            value = known(src[pl.ds(at_row, CHUNK)], start + at_row).T
            high = value.astype(BF16)
            columns = pl.ds(pl.multiple_of(start + at_row, CHUNK), CHUNK)
            ahi[i, rows, columns] = high
            alo[i, rows, columns] = (value - high.astype(F32)).astype(BF16)
            return 0

        lax.fori_loop(0, size // CHUNK, step, 0)

    def take_v(s, half):
        sized(half * PART, PART, x, lambda local, _: wait(vx.at[s, local], grecv_v.at[s, half]))
        if s < 2:
            forward(s, half)

    def forward_last(side):
        lanes = pl.ds(side * LANES, LANES)
        remote(vx.at[2, :, lanes], vz.at[3, :, lanes], fsend.at[3, side], frecv.at[3, side], at(dzl=1))

    def take_last(side):
        lanes = pl.ds(side * LANES, LANES)
        wait(vz.at[3, :, lanes], frecv.at[3, side])
        split_v(vz.at[3, :, lanes], 7, 0, QUARTER, lanes)

    def split_taken(s, half):
        split_v(vx.at[s, pl.ds(half * PART, PART)], s + 1, half * PART, PART)

    def take_z(s, half):
        rows = pl.ds(half * PART, PART)
        if s == 0:
            sized(half * PART, PART, x, lambda local, _: wait(vz.at[s, local], frecv.at[s, half]))
        else:
            wait(vz.at[s, rows], frecv.at[s, half])
        split_v(vz.at[s, rows], 4 + s, half * PART, PART)

    def take_a(s, half):
        sized(half * PART, PART, x, lambda local, _: wait(ax.at[s, local], grecv_a.at[s, half]))
        split_a(ax.at[s, pl.ds(half * PART, PART)], s + 1, 0, half * PART, PART)

    def take_far(side):
        for way in range(2):
            sized(way * PART, PART, x, lambda local, _: wait(afar.at[side, local], far_recv.at[side, way]))
        split_a(afar.at[side], 3, side * HALF, 0, QUARTER)

    def load_v(u, act):
        sized(u * UNIT, UNIT, x, lambda local, whole: act(
            itg.at[whole], stage_v.at[u % 2, pl.ds(0, local.size)], own_v.at[u % 2]))

    def load_a(u, act):
        sized(u % 4 * UNIT, UNIT, x if u < 4 else quarter_of(2), lambda local, whole: act(
            amp.at[whole], stage_a.at[u % 2, pl.ds(0, local.size)], own_a.at[u % 2]))

    def begin(src, dst, sem):
        pltpu.make_async_copy(src, dst, sem).start()

    def end(src, dst, sem):
        wait(dst, sem)

    def set_aside(u):
        def step(c, _):
            at_row = pl.multiple_of(c * CHUNK, CHUNK)
            n = amp.shape[1] - HALF
            aside[pl.ds(pl.multiple_of(u % 4 * UNIT + at_row, CHUNK), CHUNK), pl.ds(0, n)] = stage_a[
                u % 2, pl.ds(at_row, CHUNK), pl.ds(HALF, n)
            ]
            return 0

        lax.fori_loop(0, UNIT // CHUNK, step, 0)

    def rows_of(half):
        return pl.ds(0, ROWS) if half is None else pl.ds(half * HALF, HALF)

    def sem_row(i, half):
        return i if half is None else 3 + half

    def product(i, rows, n, high_v, low_v):
        high, low = ahi[i, rows], alo[i, rows]
        both = jnp.concatenate([high, low], axis=0)
        one = dot(both, high_v)
        if n == ROWS:
            return one[:n] + one[n:] + dot(high, low_v)
        two = dot(both, low_v)
        return one[:n] + one[n:] + two[:n] + two[n:]

    def produce(i, j, half, slot):
        rows = rows_of(half)
        n = ROWS if half is None else HALF
        value = product(i, rows, n, vhi[j], vlo[j])
        ptile[slot, 0, pl.ds(0, n)] = value[:, :LANES]
        ptile[slot, 1, pl.ds(0, n)] = value[:, LANES:]
        remote(
            ptile.at[slot, 1 - core, pl.ds(0, n)], crecv.at[j, i, rows],
            csend.at[slot], crecv_sem.at[j, sem_row(i, half)], at(dc=1),
        )

    def finish(i, j, half, own):
        rows = rows_of(half)
        n = ROWS if half is None else HALF
        wait(crecv.at[j, i, rows], crecv_sem.at[j, sem_row(i, half)])
        crecv[j, i, rows] += own[pl.ds(0, n)]
        d, zj = lax.rem(j, 4), j // 4
        shift = jnp.where(d == 0, 4, jnp.where(d == 1, 3, jnp.where(d == 2, 5, 6)))
        target = lax.rem(x + shift, 4)
        distance = lax.rem(y - target + 4, 4)

        @pl.when(distance != 0)
        def _():
            remote(
                crecv.at[j, i, rows], yrecv.at[distance - 1, zj, i, rows],
                ysend, yrecv_sem.at[distance - 1, zj, sem_row(i, half)],
                (occ, zh * 8 + target * 2 + core),
            )

    def tiles(count, n, index, half=None, free=0):
        def step(k, _):
            @pl.when(k < n)
            def _():
                i, j = index(k)
                slot = lax.rem(count + k, SLOTS)

                @pl.when(k >= free)
                def _():
                    wait(ptile.at[slot, 0, pl.ds(0, ROWS if half is None else HALF)], csend.at[slot])

                produce(i, j, half, slot)

            @pl.when(k > 0)
            def _():
                i, j = index(k - 1)
                finish(i, j, half, ptile.at[lax.rem(count + k - 1, SLOTS), core])

            return 0

        lax.fori_loop(0, n + 1, step, 0)

    def settle(n):
        for slot in range(SLOTS):
            wait(ptile.at[slot, 0, pl.ds(0, n)], csend.at[slot])

    def last_tiles(side, n, half=None):
        lanes = pl.ds(side * LANES, LANES)
        rows = rows_of(half)
        block = (lambda k: k) if half is None else (lambda k: 3)

        def step(k, _):
            @pl.when(k < n)
            def _():
                i = block(k)
                plast[side, i, rows] = product(i, rows, ROWS if half is None else HALF, vhi[7, :, lanes], vlo[7, :, lanes])

                @pl.when(core != side)
                def _():
                    remote(
                        plast.at[side, i, rows], crecv.at[7, i, rows],
                        lsend.at[side, sem_row(i, half)], crecv_sem.at[7, sem_row(i, half)], at(dc=1),
                    )

            @pl.when((k > 0) & (core == side))
            def _():
                i = block(k - 1)
                finish(i, 7, half, plast.at[side, i, rows])

            return 0

        lax.fori_loop(0, n + 1, step, 0)

    for half in range(2):
        send_near("v", half)
        sized(half * PART, PART, x, lambda local, whole, half=half: remote(
            itg.at[whole], vz.at[0, local], fsend.at[0, half], frecv.at[0, half], at(dzl=1)))
    for way in range(2):
        start_v(way)
    send_near("a", 0)
    send_near("a", 1)
    for u in range(2):
        load_v(u, begin)
        load_a(u, begin)
    for u in range(4):
        load_v(u, end)
        split_v(stage_v.at[u % 2], 0, u * UNIT, UNIT)
        if u < 2:
            load_v(u + 2, begin)
    for u in range(8):
        load_a(u, end)
        if u < 4:
            split_a(stage_a.at[u % 2], 0, 0, u * UNIT, UNIT)
        else:
            set_aside(u)
        if u < 6:
            load_a(u + 2, begin)

    take_v(0, 0)
    take_v(1, 0)
    split_taken(0, 0)
    split_taken(1, 0)
    take_z(0, 0)

    take_v(0, 1)
    take_v(1, 1)
    split_taken(0, 1)
    split_taken(1, 1)
    take_z(0, 1)
    tiles(0, 4, lambda k: (0, k + k // 3), free=4)

    take_a(0, 0)
    take_a(1, 0)
    take_z(1, 0)

    for way in range(2):
        pass_v(way)
    for side in range(2):
        for way in range(2):
            start_a(side, way)
    take_z(2, 0)

    take_a(0, 1)
    take_a(1, 1)
    tiles(4, 8, lambda k: (1 + k // 4, k % 4 + k % 4 // 3))
    take_z(1, 1)
    tiles(12, 3, lambda k: (k, 5))

    take_v(2, 0)
    take_v(2, 1)
    forward_last(0)
    forward_last(1)
    split_taken(2, 0)
    split_taken(2, 1)
    tiles(15, 3, lambda k: (k, 3))
    take_z(2, 1)
    tiles(18, 3, lambda k: (k, 6))

    mine = lax.rem(y - x + 4, 4)
    mine = jnp.where(mine == 0, 0, jnp.where(mine == 3, 1, jnp.where(mine == 1, 2, 3)))

    def collect(zj, i, half=None):
        row = sem_row(i, half)
        start = 0 if half is None else half * HALF
        for s in range(3):
            wait(yrecv.at[s, zj, i, rows_of(half)], yrecv_sem.at[s, zj, row])

        def step(c, _):
            rows = pl.ds(pl.multiple_of(start + c * 32, 32), 32)
            total[zj, i, rows] = (crecv[zj * 4 + mine, i, rows] + yrecv[0, zj, i, rows]) + (
                yrecv[1, zj, i, rows] + yrecv[2, zj, i, rows]
            )
            return 0

        lax.fori_loop(0, (ROWS if half is None else HALF) // 32, step, 0)
        if i > 0:
            s, rows = (None, 1, 0, 2)[i], rows_of(half)
            remote(
                total.at[zj, i, rows], xrecv.at[s, zj, rows],
                osend.at[row - 1, zj], orecv.at[row - 1, zj], at(dx=OFFSET[i]),
            )

    late = mine == 3

    for way in range(2):
        pass_a(0, way)
    for way in range(2):
        pass_a(1, way)

    for i in (1, 2, 0):
        collect(0, i)

    @pl.when(~late)
    def _():
        for i in (1, 2, 0):
            collect(1, i)

    take_last(0)
    last_tiles(0, 3)
    take_far(0)
    settle(ROWS)
    tiles(0, 7, lambda k: (3, k), half=0, free=SLOTS)
    last_tiles(0, 1, half=0)
    collect(0, 3, 0)

    @pl.when(~late)
    def _():
        collect(1, 3, 0)

    @pl.when(late & (core == 0))
    def _():
        for i in (1, 2, 0):
            collect(1, i)
        collect(1, 3, 0)

    settle(HALF)
    take_last(1)
    last_tiles(1, 3)
    last_tiles(1, 1, half=0)
    take_far(1)
    tiles(0, 8, lambda k: (3, k), half=1, free=SLOTS)

    @pl.when(late & (core == 1))
    def _():
        for i in (1, 2, 0):
            collect(1, i)
        collect(1, 3, 0)

    collect(0, 3, 1)
    collect(1, 3, 1)

    keep = lax.rem(zl + zh, 2)
    parts = [(i, None) for i in (1, 2)] + [(3, half) for half in range(2)]
    def arrived(zj, some):
        for i, half in some:
            wait(xrecv.at[(None, 1, 0, 2)[i], zj, rows_of(half)], orecv.at[sem_row(i, half) - 1, zj])

    def summed(zj, rows):
        return (total[zj, 0, rows] + xrecv[0, zj, rows]) + (xrecv[1, zj, rows] + xrecv[2, zj, rows])

    for half in range(2):
        rows = rows_of(half)
        arrived(1 - keep, parts[:3] if half == 0 else parts[3:])
        zsend[rows] = summed(1 - keep, rows)
        remote(zsend.at[rows], zrecv.at[rows], zsem.at[0, half], zsem.at[1, half], at(dzh=1))
    arrived(keep, parts)
    result = summed(keep, rows_of(None))[: out.shape[0]]
    for half in range(2):
        wait(zrecv.at[rows_of(half)], zsem.at[1, half])
    out[...] = result + zrecv[: out.shape[0]]

    for half in range(2):
        wait(zsend.at[rows_of(half)], zsem.at[0, half])
    wait(yrecv, ysend)
    settle(HALF)
    for zj in range(2):
        for i, half in parts:
            wait(total.at[zj, i, rows_of(half)], osend.at[sem_row(i, half) - 1, zj])
    for side in range(2):

        @pl.when(core != side)
        def _():
            for i, half in [(0, None)] + parts[:3]:
                wait(plast.at[side, i, rows_of(half)], lsend.at[side, sem_row(i, half)])

    for half in range(2):
        for s, dx in enumerate((1, -1)):
            sized(half * PART, PART, quarter_of(dx), lambda local, _: wait(vx.at[s, local], gsend.at[s, half]))
            sized(half * PART, PART, quarter_of(dx), lambda local, _: wait(ax.at[s, local], gsend.at[s, 2 + half]))
        way = half
        sized(way * PART, PART, quarter_of(2), lambda local, _: wait(vx.at[2, local], hsend_v.at[way]))
        sized(way * PART, PART, quarter_of(1 - 2 * way), lambda local, _: wait(vx.at[2, local], rsend_v.at[way]))
        for side in range(2):
            sized(way * PART, PART, quarter_of(2), lambda local, _: wait(afar.at[side, local], hsend_a.at[side, way]))
            sized(way * PART, PART, quarter_of(1 - 2 * way), lambda local, _: wait(afar.at[side, local], rsend_a.at[side, way]))
    for half in range(2):
        sized(half * PART, PART, x, lambda local, _: wait(vz.at[0, local], fsend.at[0, half]))
        for s in range(1, 4):
            wait(vz.at[s, pl.ds(half * PART, PART)], fsend.at[s, half])


def body(integrals, amplitudes, residual_in):
    rows = amplitudes.shape[0]
    any_spec = pl.BlockSpec(memory_space=pl.ANY)
    vmem_spec = pl.BlockSpec(memory_space=pltpu.VMEM)
    dma = pltpu.SemaphoreType.DMA
    ladder = pl.pallas_call(
        kernel,
        name="ladder",
        out_shape=(
            jax.ShapeDtypeStruct(residual_in.shape, F32),
            jax.ShapeDtypeStruct((2, PART, ROWS), F32),
            jax.ShapeDtypeStruct((2, 2, PART, HALF), F32),
        ),
        in_specs=[any_spec] * 2,
        out_specs=(vmem_spec, any_spec, any_spec),
        scratch_shapes=[
            pltpu.VMEM((3, QUARTER, ROWS), F32),
            pltpu.VMEM((4, QUARTER, ROWS), F32),
            pltpu.VMEM((2, QUARTER, rows), F32),
            pltpu.VMEM((2, QUARTER, HALF), F32),
            pltpu.VMEM((QUARTER, HALF), F32),
            pltpu.VMEM((2, UNIT, ROWS), F32),
            pltpu.VMEM((2, UNIT, rows), F32),
            pltpu.VMEM((8, QUARTER, ROWS), BF16),
            pltpu.VMEM((8, QUARTER, ROWS), BF16),
            pltpu.VMEM((4, ROWS, QUARTER), BF16),
            pltpu.VMEM((4, ROWS, QUARTER), BF16),
            pltpu.VMEM((SLOTS, 2, ROWS, LANES), F32),
            pltpu.VMEM((2, 4, ROWS, LANES), F32),
            pltpu.VMEM((8, 4, ROWS, LANES), F32),
            pltpu.VMEM((3, 2, 4, ROWS, LANES), F32),
            pltpu.VMEM((3, 2, ROWS, LANES), F32),
            pltpu.VMEM((2, 4, ROWS, LANES), F32),
            pltpu.VMEM((ROWS, LANES), F32),
            pltpu.VMEM((ROWS, LANES), F32),
            dma((2,)),
            dma((2,)),
            dma((2, 4)),
            dma((3, 2)),
            dma((2, 2)),
            dma((2,)),
            dma((2,)),
            dma((2, 2)),
            dma((2, 2)),
            dma((2,)),
            dma((2, 2)),
            dma((2, 2)),
            dma((4, 2)),
            dma((4, 2)),
            dma((SLOTS,)),
            dma((2, 5)),
            dma((8, 5)),
            dma,
            dma((3, 2, 5)),
            dma((4, 2)),
            dma((4, 2)),
            dma((2, 2)),
        ],
        compiler_params=pltpu.CompilerParams(
            collective_id=0, has_side_effects=True, vmem_limit_bytes=61 * 2**20
        ),
        cost_estimate=pl.CostEstimate(flops=3 * 2 * 1008 * 2048 * 2048, bytes_accessed=2 * 2**24, transcendentals=0),
    )(amplitudes.T, integrals.T)[0]
    return residual_in + ladder


def solution(mesh):
    return jax.shard_map(
        body,
        mesh=mesh,
        in_specs=(P("occ", "vir"), P("occ", "vir"), P("occ", "vir")),
        out_specs=P("occ", "vir"),
        check_vma=False,
    )
```
